32 devices in a mesh: row: 8 (over z, core), col: 4 (over y, x).
Axes of the slice: x: 2, y: 2, z: 4, core: 2. Of those that a mesh axis runs over, the one named last changes fastest.
Arguments:
- pressure_in: float32 [256, 64, 128], P('row', 'col'), may hold values from -6 to 6
- source: float32 [256, 64, 128], P('row', 'col'), may hold values from -18 to 18
- permeability: float32 [256, 64, 128], P('row', 'col'), may hold values from 0.2 to 5
Outputs:
- pressure_out: float32 [256, 64, 128], P('row', 'col')
The draws below stay inside these ranges and needn't reach their ends.
All inputs are finite; a program needn't handle non-finite values.
Results may differ from the reference program's by a relative error of at most 0.0001.
Values sent between devices are 32-bit elements; how exact they have to be, the bound alone decides.
A program may use at most 128 MiB of HBM per device.

```python
import math
import jax
import jax.numpy as jnp

NZ = 128
LEVELS = 3
NU1 = 2
NU2 = 2
CSWEEPS = 16
NX = 256
NY = 64


def steps_of(own_key, dims, split, least, high):
    factor_of, own = 1.0, jax.random.fold_in(own_key, 6)
    for dim, shards_of in split:
        steps = jnp.exp(jax.random.uniform(jax.random.fold_in(own, dim), (shards_of,), jnp.float32, least / len(split), high / len(split)))
        factor_of = factor_of * jnp.repeat(steps, dims[dim] // shards_of).reshape([-1 if axis == dim else 1 for axis in range(len(dims))])
    return factor_of


def gaussian(stream_key, extent, deviation, bound, shards=(), kind=jnp.bfloat16):
    gain = steps_of(stream_key, extent, shards, -0.22, 0.18) if shards else 1.0
    values = jax.random.normal(stream_key, extent, jnp.float32) * deviation * gain
    return jnp.minimum(jnp.maximum(values, -bound), bound).astype(kind)


def setup_inputs(seed: int = 0) -> dict:
    keys = jax.random.split(jax.random.key(seed), 4)
    pressure_in = gaussian(keys[0], (NX, NY, NZ), 1.0, 6.0, ((0, 8), (1, 4)), jnp.float32)
    source = gaussian(keys[1], (NX, NY, NZ), 3.0, 18.0, ((0, 8), (1, 4)), jnp.float32)
    permeability = jnp.clip(jnp.exp(math.log(5.0) - 3.218876 * jax.random.uniform(keys[2], (NX, NY, NZ), jnp.float32) ** steps_of(keys[2], (NX, NY, NZ), ((0, 8), (1, 4)), -0.2, 0.2)), 0.2, 5.0)
    return dict(pressure_in=pressure_in, source=source, permeability=permeability)


OMEGA = 0.8


def harmonic(left, right, scale):
    return 2.0 * left * right / (left + right) * scale


def coefficients(padded, center, scale):
    west_x = harmonic(padded[:-2, 1:-1], center, scale)
    east_x = harmonic(center, padded[2:, 1:-1], scale)
    west_y = harmonic(padded[1:-1, :-2], center, scale)
    east_y = harmonic(center, padded[1:-1, 2:], scale)
    inner = harmonic(center[:, :, :-1], center[:, :, 1:], scale)
    below = jnp.concatenate([2.0 * center[:, :, :1] * scale, inner], axis=2)
    above = jnp.concatenate([inner, 2.0 * center[:, :, -1:] * scale], axis=2)
    diagonal = west_x + east_x + west_y + east_y + below + above
    return (west_x, east_x, west_y, east_y, below, above, diagonal)


def apply_operator(padded, center, faces):
    west_x, east_x, west_y, east_y, below, above, diagonal = faces
    zero_plane = jnp.zeros_like(center[:, :, :1])
    under = jnp.concatenate([zero_plane, center[:, :, :-1]], axis=2)
    over = jnp.concatenate([center[:, :, 1:], zero_plane], axis=2)
    beside_all = west_x * padded[:-2, 1:-1] + east_x * padded[2:, 1:-1]
    beside_all = beside_all + west_y * padded[1:-1, :-2] + east_y * padded[1:-1, 2:]
    beside_all = beside_all + below * under + above * over
    return diagonal * center - beside_all


def jacobi_sweep(pressure, right_side, faces, padder):
    return pressure + OMEGA * (right_side - apply_operator(padder(pressure), pressure, faces)) / faces[6]


def first_sweep(right_side, faces):
    return OMEGA * right_side / faces[6]


def coarsen(field):
    size_x, size_y, size_z = field.shape
    return field.reshape(size_x // 2, 2, size_y // 2, 2, size_z // 2, 2).mean(axis=(1, 3, 5))


def prolong(field):
    return jnp.repeat(jnp.repeat(jnp.repeat(field, 2, axis=0), 2, axis=1), 2, axis=2)


def wrap_pad(field):
    return jnp.pad(field, ((1, 1), (1, 1), (0, 0)), mode="wrap")


def reference(pressure_in, source, permeability):
    perms = [permeability]
    for depth_level in range(LEVELS):
        perms.append(coarsen(perms[-1]))
    all_faces = [coefficients(wrap_pad(perms[depth_level]), perms[depth_level], 0.25 ** depth_level) for depth_level in range(LEVELS + 1)]
    pressure = pressure_in
    right_side = source
    states = []
    for depth_level in range(LEVELS):
        faces = all_faces[depth_level]
        if depth_level == 0:
            for sweep_index in range(NU1):
                pressure = jacobi_sweep(pressure, right_side, faces, wrap_pad)
        else:
            pressure = first_sweep(right_side, faces)
            for sweep_index in range(NU1 - 1):
                pressure = jacobi_sweep(pressure, right_side, faces, wrap_pad)
        states.append((pressure, right_side))
        residual = right_side - apply_operator(wrap_pad(pressure), pressure, faces)
        right_side = coarsen(residual)
    faces = all_faces[LEVELS]
    correction = first_sweep(right_side, faces)
    for sweep_index in range(CSWEEPS - 1):
        correction = jacobi_sweep(correction, right_side, faces, wrap_pad)
    for depth_level in range(LEVELS - 1, -1, -1):
        pressure, right_side = states[depth_level]
        pressure = pressure + prolong(correction)
        for sweep_index in range(NU2):
            pressure = jacobi_sweep(pressure, right_side, all_faces[depth_level], wrap_pad)
        correction = pressure
    return correction
```

```python
import functools

import jax
import jax.numpy as jnp
from jax import lax
from jax.experimental import pallas as pl
from jax.experimental.pallas import tpu as pltpu
from jax.sharding import PartitionSpec as P

MESH = pl.DeviceIdType.MESH
OMEGA = 0.8
CSWEEPS = 16
PAD = 4


def lane_ids(rows):
    return lax.broadcasted_iota(jnp.int32, (rows, 128), 1)


def row_ids(rows):
    return lax.broadcasted_iota(jnp.int32, (rows, 128), 0)


def roll(value, shift, axis):
    return pltpu.roll(value, shift % value.shape[axis], axis)


def harmonic(left, right, scale):
    return (2.0 * scale) * left * right / (left + right)


def pair_sum(value, step):
    low = (lane_ids(value.shape[0]) // step) % 2 == 0
    return value + jnp.where(low, roll(value, -step, 1), roll(value, step, 1))


class Window:
    def __init__(self, nx, ny, step, scale):
        self.nx, self.ny, self.sub, self.step, self.scale = nx, ny, ny + 2 * PAD, step, scale

    def at(self, x):
        start = x * self.sub
        if not isinstance(x, int):
            start = pl.multiple_of(start, 8)
        return pl.ds(start, self.sub)

    def faces(self, perm, cx, cy, cz, diag, weight, lo, hi):
        lane = lane_ids(self.sub)

        def west(x, carry):
            cx[self.at(x), :] = harmonic(perm[self.at(x - 1), :], perm[self.at(x), :], self.scale)
            return carry

        lax.fori_loop(lo, hi + 1, west, 0)

        def cell(x, carry):
            k = perm[self.at(x), :]
            south = harmonic(roll(k, 1, 0), k, self.scale)
            under = jnp.where(lane < self.step, 0.0, harmonic(roll(k, self.step, 1), k, self.scale))
            outer = 2.0 * k * self.scale
            below = jnp.where(lane < self.step, outer, under)
            above = jnp.where(lane >= 128 - self.step, outer, roll(under, -self.step, 1))
            total = cx[self.at(x), :] + cx[self.at(x + 1), :] + south + roll(south, -1, 0)
            total = total + below + above
            cy[self.at(x), :] = south
            cz[self.at(x), :] = under
            diag[self.at(x), :] = total
            weight[self.at(x), :] = OMEGA / total
            return carry

        lax.fori_loop(lo, hi, cell, 0)

    def beside(self, x, v, cx, cy, cz):
        own = v[self.at(x), :]
        south, under = cy[self.at(x), :], cz[self.at(x), :]
        total = cx[self.at(x), :] * v[self.at(x - 1), :] + cx[self.at(x + 1), :] * v[self.at(x + 1), :]
        total = total + (south * roll(own, 1, 0) + roll(south * own, -1, 0))
        total = total + (under * roll(own, self.step, 1) + roll(under * own, -self.step, 1))
        return own, total

    def sweep(self, v, rhs, faces, lo, hi, store):
        cx, cy, cz, _, weight = faces

        def body(x, carry):
            own, total = self.beside(x, v, cx, cy, cz)
            store(x, (1.0 - OMEGA) * own + weight[self.at(x), :] * (rhs[self.at(x), :] + total))
            return carry

        lax.fori_loop(lo, hi, body, 0, unroll=2)

    def residual(self, x, v, rhs, faces):
        cx, cy, cz, diag, _ = faces
        own, total = self.beside(x, v, cx, cy, cz)
        return rhs[self.at(x), :] - diag[self.at(x), :] * own + total


class Packed:
    def __init__(self, rows, cols, level):
        self.rows, self.cols, self.level = rows, cols, level
        self.sub = cols * 8
        self.scale = 0.25**level
        self.ystep, self.zstep = (2, 4) if level == 2 else (4, 8)

    def at(self, r):
        return pl.ds(pl.multiple_of(r * self.sub, 8), self.sub)

    def prev(self, r):
        return lax.rem(r + self.rows - 1, self.rows)

    def next(self, r):
        return lax.rem(r + 1, self.rows)

    def west(self, here, before):
        j = lane_ids(self.sub) % 4
        if self.level == 3:
            return jnp.where(j > 0, roll(here, 1, 1), roll(before, -3, 1))
        odd = row_ids(self.sub) % 2 == 1
        up, up_before = roll(here, -1, 0), roll(before, -1, 0)
        other = jnp.where(j > 0, roll(up, 1, 1), roll(up_before, -3, 1))
        return jnp.where(odd, roll(here, 1, 0), other)

    def east(self, here, after):
        j = lane_ids(self.sub) % 4
        if self.level == 3:
            return jnp.where(j < 3, roll(here, -1, 1), roll(after, 3, 1))
        odd = row_ids(self.sub) % 2 == 1
        down, down_after = roll(here, 1, 0), roll(after, 1, 0)
        other = jnp.where(j < 3, roll(down, -1, 1), roll(down_after, 3, 1))
        return jnp.where(odd, other, roll(here, -1, 0))

    def loop(self, body):
        def step(r, carry):
            body(r)
            return carry

        lax.fori_loop(0, self.rows, step, 0, unroll=2)

    def faces(self, perm, cx, cy, cz, diag, weight):
        lane = lane_ids(self.sub)

        def first(r):
            k = perm[self.at(r), :]
            cx[self.at(r), :] = harmonic(self.west(k, perm[self.at(self.prev(r)), :]), k, self.scale)

        self.loop(first)

        def second(r):
            k = perm[self.at(r), :]
            lower = cx[self.at(r), :]
            south = harmonic(roll(k, self.ystep, 0), k, self.scale)
            under = harmonic(roll(k, self.zstep, 1), k, self.scale)
            under = jnp.where(lane < self.zstep, 0.0, under)
            outer = 2.0 * k * self.scale
            below = jnp.where(lane < self.zstep, outer, under)
            above = jnp.where(lane >= 128 - self.zstep, outer, roll(under, -self.zstep, 1))
            total = lower + self.east(lower, cx[self.at(self.next(r)), :])
            total = total + south + roll(south, -self.ystep, 0) + below + above
            cy[self.at(r), :] = south
            cz[self.at(r), :] = under
            diag[self.at(r), :] = total
            weight[self.at(r), :] = OMEGA / total

        self.loop(second)

    def beside(self, r, v, cx, cy, cz):
        own = v[self.at(r), :]
        lower, south, under = cx[self.at(r), :], cy[self.at(r), :], cz[self.at(r), :]
        before, after = self.at(self.prev(r)), self.at(self.next(r))
        total = lower * self.west(own, v[before, :])
        total = total + self.east(lower * own, cx[after, :] * v[after, :])
        total = total + (south * roll(own, self.ystep, 0) + roll(south * own, -self.ystep, 0))
        total = total + (under * roll(own, self.zstep, 1) + roll(under * own, -self.zstep, 1))
        return own, total

    def start(self, v, rhs, weight):
        def body(r):
            v[self.at(r), :] = weight[self.at(r), :] * rhs[self.at(r), :]

        self.loop(body)

    def sweep(self, v, new, rhs, faces):
        cx, cy, cz, _, weight = faces

        def body(r):
            own, total = self.beside(r, v, cx, cy, cz)
            update = weight[self.at(r), :] * (rhs[self.at(r), :] + total)
            new[self.at(r), :] = (1.0 - OMEGA) * own + update

        self.loop(body)

    def block_mean(self, value):
        row = row_ids(self.sub)
        value = value + jnp.where(row % 2 == 0, roll(value, -1, 0), roll(value, 1, 0))
        value = value + jnp.where(row // 2 % 2 == 0, roll(value, -2, 0), roll(value, 2, 0))
        return pair_sum(value, 4) * 0.125


class Exchange:
    def __init__(self, win, items, bufs, sems, base, ids):
        self.win, self.items, self.ids = win, items, ids
        self.ystage, self.yland, self.cstage, self.cland = bufs
        self.sems, self.base = sems, base
        self.layers = sum(h for _, h in items)

    def remote(self, src, dst, to):
        send, recv = self.sems
        copy = pltpu.make_async_remote_copy(
            src_ref=src, dst_ref=dst, send_sem=send.at[self.base], recv_sem=recv.at[self.base],
            device_id=to, device_id_type=MESH)
        self.base += 1
        copy.start()
        return copy

    def edge(self, h, side, i):
        ny, sub = self.win.ny, self.win.sub
        return (i, ny + i) if side == 0 else (ny - h + i, sub - h + i)

    def spans(self, h):
        return (PAD - h, PAD + self.win.nx)

    def start(self):
        (me_r, me_c), (left, right), (down, up) = self.ids
        nx, sub = self.win.nx, self.win.sub
        self.x_copies = []
        for ref, h in self.items:
            rows = h * sub
            lower, upper = PAD * sub, (PAD + nx - h) * sub
            self.x_copies.append(self.remote(
                ref.at[pl.ds(lower, rows), :], ref.at[pl.ds((PAD + nx) * sub, rows), :], (left, me_c)))
            self.x_copies.append(self.remote(
                ref.at[pl.ds(upper, rows), :], ref.at[pl.ds((PAD - h) * sub, rows), :], (right, me_c)))
        self.y_copies = []
        for side, to in ((0, down), (1, up)):
            n = 0
            for ref, h in self.items:
                for i in range(h):
                    mine, _ = self.edge(h, side, i)
                    self.ystage[side, n * nx:(n + 1) * nx, :] = ref[pl.ds(PAD * sub + mine, nx, stride=sub), :]
                    n += 1
            self.y_copies.append(self.remote(self.ystage.at[side], self.yland.at[side], (me_r, to)))

    def corners(self):
        (me_r, me_c), _, (down, up) = self.ids
        sub = self.win.sub
        for copy in self.x_copies:
            copy.wait()
        self.c_copies = []
        for side, to in ((0, down), (1, up)):
            n = 0
            for ref, h in self.items:
                for i in range(h):
                    mine, _ = self.edge(h, side, i)
                    for first in self.spans(h):
                        for x in range(first, first + h):
                            self.cstage[side, n:n + 1, :] = ref[pl.ds(x * sub + mine, 1), :]
                            n += 1
            self.c_copies.append(self.remote(self.cstage.at[side], self.cland.at[side], (me_r, to)))

    def finish(self):
        nx, sub = self.win.nx, self.win.sub
        for copy in self.y_copies:
            copy.wait()
        for copy in self.c_copies:
            copy.wait()
        for side in (0, 1):
            n, m = 0, 0
            for ref, h in self.items:
                for i in range(h):
                    _, halo = self.edge(h, side, i)
                    ref[pl.ds(PAD * sub + halo, nx, stride=sub), :] = self.yland[side, n * nx:(n + 1) * nx, :]
                    n += 1
                    for first in self.spans(h):
                        for x in range(first, first + h):
                            ref[pl.ds(x * sub + halo, 1), :] = self.cland[side, m:m + 1, :]
                            m += 1


def stage_sizes(win, halos):
    layers = sum(halos)
    corner = sum(2 * h * h for h in halos)
    corner = (corner + 7) // 8 * 8
    return [(2, layers * win.nx, 128)] * 2 + [(2, corner, 128)] * 2


def gather(src, land, tiles, sems, sizes, ids):
    rows, cols = sizes
    (me_r, me_c), _, _ = ids
    send, recv = sems

    def one(k, carry):
        to = (lax.rem(me_r + rows - k // cols, rows), lax.rem(me_c + cols - k % cols, cols))
        pltpu.make_async_remote_copy(
            src_ref=src, dst_ref=land.at[pl.ds(pl.multiple_of(k * 8, 8), 8), :], send_sem=send,
            recv_sem=recv, device_id=to, device_id_type=MESH).start()
        return carry

    lax.fori_loop(1, tiles, one, 0)


def gather_wait(land, tiles, sems, ids):
    (me_r, me_c), (left, _), _ = ids
    span = land.at[pl.ds(8, (tiles - 1) * 8), :]
    done = pltpu.make_async_remote_copy(
        src_ref=span, dst_ref=span, send_sem=sems[0], recv_sem=sems[1],
        device_id=(left, me_c), device_id_type=MESH)
    done.wait_send()
    done.wait_recv()


def cycle_kernel(sizes, wins, p_in, s_in, k_in, out, *scratch):
    rows, cols = sizes
    tiles = rows * cols
    fine, mid = wins
    scratch = list(scratch)

    def take(count):
        got, scratch[:count] = scratch[:count], []
        return got

    pw, pa, pb, sw, kw, vw = take(6)
    faces0 = take(5)
    b1, k1, va, vb, v1 = take(5)
    faces1 = take(5)
    k2, b2, p2a, p2b = take(4)
    faces2 = take(5)
    b3, p3a, p3b = take(3)
    faces3 = take(5)
    tmp, tile_b, tile_k = take(3)
    x0, x1, x2, x3 = take(4), take(4), take(4), take(4)
    send, recv, gsend, grecv = take(4)

    me_r, me_c = lax.axis_index("row"), lax.axis_index("col")
    ids = ((me_r, me_c),
           (lax.rem(me_r + rows - 1, rows), lax.rem(me_r + 1, rows)),
           (lax.rem(me_c + cols - 1, cols), lax.rem(me_c + 1, cols)))

    barrier = pltpu.get_barrier_semaphore()

    def greet(k, carry):
        to = (lax.rem(me_r + k // cols, rows), lax.rem(me_c + k % cols, cols))
        pl.semaphore_signal(barrier, inc=1, device_id=to, device_id_type=MESH)
        return carry

    lax.fori_loop(1, tiles, greet, 0)

    nx, ny, sub = fine.nx, fine.ny, fine.sub

    def bring(x, carry):
        at = pl.ds(pl.multiple_of((x + PAD) * sub, 8), ny)
        kw[at, :] = k_in[x]
        pw[at, :] = p_in[x]
        sw[at, :] = s_in[x]
        return carry

    lax.fori_loop(0, nx, bring, 0, unroll=2)
    pl.semaphore_wait(barrier, tiles - 1)

    first = Exchange(fine, [(kw, 3), (pw, 3), (sw, 2)], x0, (send, recv), 0, ids)
    first.start()

    def k_mean(i, carry):
        x = 2 * i
        total = pair_sum(k_in[x] + k_in[x + 1], 1)
        tmp[0:ny, :] = total
        halves = tmp[pl.ds(0, ny // 2, stride=2), :] + tmp[pl.ds(1, ny // 2, stride=2), :]
        k1[pl.ds(pl.multiple_of((i + PAD) * mid.sub, 8), mid.ny), :] = halves * 0.125
        return carry

    lax.fori_loop(0, nx // 2, k_mean, 0)
    first.corners()

    def to_tile(row_of, tile):
        lane = lane_ids(mid.ny // 2)
        packs = [None, None]
        for x in range(mid.nx // 2):
            j, i = x // 2, x % 2
            total = pair_sum(row_of(2 * x + PAD) + row_of(2 * x + 1 + PAD), 2)
            tmp[0:mid.sub, :] = total
            n = mid.ny // 2
            block = (tmp[pl.ds(0, n, stride=2), :] + tmp[pl.ds(1, n, stride=2), :]) * 0.125
            packs[i] = block if j == 0 else jnp.where(lane % 4 == j, block, packs[i])
        for i in range(2):
            tile[pl.ds(i, mid.ny // 2, stride=2), :] = packs[i]

    to_tile(lambda x: k1[mid.at(x), :], tile_k)
    k2[0:8, :] = tile_k[...]
    gather(tile_k, k2, tiles, (gsend.at[0], grecv.at[0]), sizes, ids)

    first.finish()
    second = Exchange(mid, [(k1, 3)], x1, (send, recv), first.base, ids)
    second.start()

    lo, hi = PAD, PAD + nx
    fine.faces(kw, *faces0, lo - 2, hi + 2)

    def put(win, ref):
        def store(x, value):
            ref[win.at(x), :] = value
        return store

    def put_both(x, value):
        pb[fine.at(x), :] = value

    fine.sweep(pw, sw, faces0, lo - 2, hi + 2, put(fine, pa))
    fine.sweep(pa, sw, faces0, lo - 1, hi + 1, put_both)

    def restrict0(i, carry):
        x = 2 * i + PAD
        total = fine.residual(x, pb, sw, faces0) + fine.residual(x + 1, pb, sw, faces0)
        tmp[0:sub, :] = pair_sum(total, 1)
        halves = tmp[pl.ds(0, ny // 2, stride=2), :] + tmp[pl.ds(1, ny // 2, stride=2), :]
        b1[pl.ds(pl.multiple_of((i + PAD) * mid.sub, 8), mid.ny), :] = halves * 0.125
        return carry

    lax.fori_loop(0, nx // 2, restrict0, 0)
    second.corners()

    third = Exchange(mid, [(b1, 2)], x2, (send, recv), second.base, ids)
    third.start()

    def keep0(x, carry):
        vw[fine.at(x), :] = pb[fine.at(x), :]
        return carry

    lax.fori_loop(lo, hi, keep0, 0, unroll=2)
    second.finish()
    lo1, hi1 = PAD, PAD + mid.nx
    mid.faces(k1, *faces1, lo1 - 2, hi1 + 2)
    third.corners()
    third.finish()

    def zero_sweep(x, carry):
        va[mid.at(x), :] = faces1[4][mid.at(x), :] * b1[mid.at(x), :]
        return carry

    lax.fori_loop(lo1 - 2, hi1 + 2, zero_sweep, 0)
    mid.sweep(va, b1, faces1, lo1 - 1, hi1 + 1, put(mid, vb))
    to_tile(lambda x: mid.residual(x, vb, b1, faces1), tile_b)
    b2[0:8, :] = tile_b[...]
    gather(tile_b, b2, tiles, (gsend.at[1], grecv.at[1]), sizes, ids)

    def keep1(x, carry):
        v1[mid.at(x), :] = vb[mid.at(x), :]
        return carry

    lax.fori_loop(lo1, hi1, keep1, 0)
    fourth = Exchange(mid, [(v1, 3)], x3[:4], (send, recv), third.base, ids)
    fourth.start()
    fifth = Exchange(fine, [(vw, 2)], take(4), (send, recv), fourth.base + 2, ids)
    fifth.start()

    coarse2, coarse3 = Packed(rows, cols, 2), Packed(rows, cols, 3)
    gather_wait(k2, tiles, (gsend.at[0], grecv.at[0]), ids)
    coarse2.faces(k2, *faces2)

    def k_coarsest(r):
        b3[coarse3.at(r), :] = coarse2.block_mean(k2[coarse2.at(r), :])

    coarse3.loop(k_coarsest)
    coarse3.faces(b3, *faces3)
    fourth.corners()
    fifth.corners()

    gather_wait(b2, tiles, (gsend.at[1], grecv.at[1]), ids)
    coarse2.start(p2a, b2, faces2[4])
    coarse2.sweep(p2a, p2b, b2, faces2)

    def restrict2(r):
        own, total = coarse2.beside(r, p2b, *faces2[:3])
        left = b2[coarse2.at(r), :] - faces2[3][coarse2.at(r), :] * own + total
        b3[coarse3.at(r), :] = coarse2.block_mean(left)

    coarse2.loop(restrict2)
    coarse3.start(p3a, b3, faces3[4])

    def two(i, carry):
        coarse3.sweep(p3a, p3b, b3, faces3)
        coarse3.sweep(p3b, p3a, b3, faces3)
        return carry

    lax.fori_loop(0, (CSWEEPS - 1) // 2, two, 0)
    coarse3.sweep(p3a, p3b, b3, faces3)

    def correct2(r):
        p2a[coarse2.at(r), :] = p2b[coarse2.at(r), :] + p3b[coarse3.at(r), :]

    coarse2.loop(correct2)
    coarse2.sweep(p2a, p2b, b2, faces2)
    coarse2.sweep(p2b, p2a, b2, faces2)

    fourth.finish()
    span = coarse2.sub
    lane = lane_ids(span)
    for dr, j in ((-1, 3), (0, 0), (0, 1), (0, 2), (0, 3), (1, 0)):
        part = p2a[(dr % rows) * span:(dr % rows + 1) * span, :]
        part = pair_sum(pair_sum(jnp.where(lane % 4 == j, part, 0.0), 1), 2)
        wrapped = roll(part, 16 - span, 0)
        tmp[0:16, :] = jnp.where(row_ids(16) < 12, part[0:16, :], wrapped[0:16, :])
        for i in range(2):
            e = tmp[pl.ds(i, 8, stride=2), :]
            x = 2 * (8 * dr + 2 * j + i) + PAD
            for row in (x, x + 1):
                for half in range(2):
                    at = pl.ds(row * mid.sub + half, 8, stride=2)
                    va[at, :] = v1[at, :] + e
    mid.sweep(va, b1, faces1, lo1 - 2, hi1 + 2, put(mid, vb))
    mid.sweep(vb, b1, faces1, lo1 - 1, hi1 + 1, put(mid, va))

    fifth.finish()

    def correct0(r, carry):
        base = pl.multiple_of(r * mid.sub, 8)
        upper = va[pl.ds(base, mid.sub), :]
        own, low = upper[0:8, :], upper[8:16, :]
        for half in range(2):
            tmp[pl.ds(half, 8, stride=2), :] = own
            tmp[pl.ds(16 + half, 2, stride=2), :] = low[0:2, :]
            tmp[pl.ds(20 + half, 2, stride=2), :] = low[6:8, :]
        e = tmp[0:sub, :]
        for x in (2 * r - PAD, 2 * r - PAD + 1):
            pa[fine.at(x), :] = vw[fine.at(x), :] + e
        return carry

    lax.fori_loop(lo1 - 1, hi1 + 1, correct0, 0)
    fine.sweep(pa, sw, faces0, lo - 1, hi + 1, put(fine, pb))

    def give(x, value):
        out[x - PAD] = value[0:ny, :]

    fine.sweep(pb, sw, faces0, lo, hi, give)


def on_device(sizes, pressure_in, source, permeability):
    rows, cols = sizes
    nx, ny, _ = pressure_in.shape
    fine, mid = Window(nx, ny, 1, 1.0), Window(nx // 2, ny // 2, 2, 0.25)

    def window(win):
        return pltpu.VMEM(((win.nx + 2 * PAD) * win.sub, 128), jnp.float32)

    packed = pltpu.VMEM((rows * cols * 8, 128), jnp.float32)
    scratch = [window(fine)] * 11 + [window(mid)] * 10 + [packed] * 17
    scratch += [pltpu.VMEM((32, 128), jnp.float32)] + [pltpu.VMEM((8, 128), jnp.float32)] * 2
    for win, halos in ((fine, (3, 3, 2)), (mid, (3,)), (mid, (2,)), (mid, (3,))):
        scratch += [pltpu.VMEM(size, jnp.float32) for size in stage_sizes(win, halos)]
    scratch += [pltpu.SemaphoreType.DMA((40,))] * 2 + [pltpu.SemaphoreType.DMA((2,))] * 2
    scratch += [pltpu.VMEM(size, jnp.float32) for size in stage_sizes(fine, (2,))]
    vmem = pl.BlockSpec(memory_space=pltpu.VMEM)
    return pl.pallas_call(
        functools.partial(cycle_kernel, sizes, (fine, mid)),
        out_shape=jax.ShapeDtypeStruct(pressure_in.shape, jnp.float32),
        in_specs=[vmem] * 3,
        out_specs=vmem,
        scratch_shapes=scratch,
        compiler_params=pltpu.CompilerParams(
            collective_id=0, has_side_effects=True, vmem_limit_bytes=58 * 1024 * 1024),
    )(pressure_in, source, permeability)


def solution(mesh):
    sizes = (mesh.shape["row"], mesh.shape["col"])
    placed = (P("row", "col", None), P("row", "col", None), P("row", "col", None))
    return jax.shard_map(
        functools.partial(on_device, sizes), mesh=mesh, in_specs=placed,
        out_specs=P("row", "col", None), check_vma=False)
```

```python
import functools

import jax
import jax.numpy as jnp
from jax import lax
from jax.experimental import pallas as pl
from jax.experimental.pallas import tpu as pltpu
from jax.sharding import PartitionSpec as P

MESH = pl.DeviceIdType.MESH
OMEGA = 0.8
CSWEEPS = 16
PAD = 4


def lane_ids(rows):
    return lax.broadcasted_iota(jnp.int32, (rows, 128), 1)


def row_ids(rows):
    return lax.broadcasted_iota(jnp.int32, (rows, 128), 0)


def roll(value, shift, axis):
    return pltpu.roll(value, shift % value.shape[axis], axis)


def harmonic(left, right, scale):
    return (2.0 * scale) * left * right / (left + right)


def pair_sum(value, step):
    low = (lane_ids(value.shape[0]) // step) % 2 == 0
    return value + jnp.where(low, roll(value, -step, 1), roll(value, step, 1))


class Window:
    def __init__(self, nx, ny, step, scale):
        self.nx, self.ny, self.sub, self.step, self.scale = nx, ny, ny + 2 * PAD, step, scale

    def at(self, x):
        start = x * self.sub
        if not isinstance(x, int):
            start = pl.multiple_of(start, 8)
        return pl.ds(start, self.sub)

    def groups(self, lo, hi, most, body):
        count = -(-(hi - lo) // most)
        size = -(-(hi - lo) // count)

        def step(g, carry):
            start = jnp.minimum(lo + g * size, hi - size)
            body([start + i for i in range(size)])
            return carry

        lax.fori_loop(0, count, step, 0)

    def faces(self, perm, cx, cy, cz, diag, weight, lo, hi, most):
        lane = lane_ids(self.sub)

        def body(rows):
            ks = [perm[self.at(x), :] for x in [rows[0] - 1] + rows + [rows[-1] + 1]]
            west = [harmonic(k, other, self.scale) for k, other in zip(ks[:-1], ks[1:])]
            found = []
            for i, k in enumerate(ks[1:-1]):
                south = harmonic(roll(k, 1, 0), k, self.scale)
                under = harmonic(roll(k, self.step, 1), k, self.scale)
                under = jnp.where(lane < self.step, 0.0, under)
                outer = 2.0 * k * self.scale
                below = jnp.where(lane < self.step, outer, under)
                above = jnp.where(lane >= 128 - self.step, outer, roll(under, -self.step, 1))
                total = west[i] + west[i + 1] + south + roll(south, -1, 0) + below + above
                found.append((south, under, total, OMEGA / total))
            for x, lower, (south, under, total, inverse) in zip(rows, west, found):
                cx[self.at(x), :] = lower
                cy[self.at(x), :] = south
                cz[self.at(x), :] = under
                diag[self.at(x), :] = total
                weight[self.at(x), :] = inverse
            cx[self.at(rows[-1] + 1), :] = west[-1]

        self.groups(lo, hi, most, body)

    def beside(self, rows, v, cx, cy, cz):
        vs = [v[self.at(x), :] for x in [rows[0] - 1] + rows + [rows[-1] + 1]]
        west = [cx[self.at(x), :] for x in rows + [rows[-1] + 1]]
        out = []
        for i, x in enumerate(rows):
            own, south, under = vs[i + 1], cy[self.at(x), :], cz[self.at(x), :]
            total = west[i] * vs[i] + west[i + 1] * vs[i + 2]
            total = total + (south * roll(own, 1, 0) + roll(south * own, -1, 0))
            total = total + (under * roll(own, self.step, 1) + roll(under * own, -self.step, 1))
            out.append((own, total))
        return out

    def sweep(self, v, rhs, faces, lo, hi, most, store):
        cx, cy, cz, _, weight = faces

        def body(rows):
            new = [(1.0 - OMEGA) * own + weight[self.at(x), :] * (rhs[self.at(x), :] + total)
                   for x, (own, total) in zip(rows, self.beside(rows, v, cx, cy, cz))]
            for x, value in zip(rows, new):
                store(x, value)

        self.groups(lo, hi, most, body)

    def residual(self, rows, v, rhs, faces):
        cx, cy, cz, diag, _ = faces
        return [rhs[self.at(x), :] - diag[self.at(x), :] * own + total
                for x, (own, total) in zip(rows, self.beside(rows, v, cx, cy, cz))]


class Packed:
    def __init__(self, rows, cols):
        self.rows, self.cols, self.sub = rows, cols, cols * 8
        self.scale = 0.25**2

    def at(self, r):
        return pl.ds(pl.multiple_of(r * self.sub, 8), self.sub)

    def west(self, here, before):
        j = lane_ids(self.sub) % 4
        odd = row_ids(self.sub) % 2 == 1
        up, up_before = roll(here, -1, 0), roll(before, -1, 0)
        other = jnp.where(j > 0, roll(up, 1, 1), roll(up_before, -3, 1))
        return jnp.where(odd, roll(here, 1, 0), other)

    def east(self, here, after):
        j = lane_ids(self.sub) % 4
        odd = row_ids(self.sub) % 2 == 1
        down, down_after = roll(here, 1, 0), roll(after, 1, 0)
        other = jnp.where(j < 3, roll(down, -1, 1), roll(down_after, 3, 1))
        return jnp.where(odd, other, roll(here, -1, 0))

    def groups(self, body):
        size = 4 if self.rows % 4 == 0 else 1

        def step(g, carry):
            body([g * size + i for i in range(size)])
            return carry

        lax.fori_loop(0, self.rows // size, step, 0)

    def around(self, rows):
        return [lax.rem(rows[0] + self.rows - 1, self.rows)] + rows + [lax.rem(rows[-1] + 1, self.rows)]

    def faces(self, perm, cx, cy, cz, diag, weight):
        lane = lane_ids(self.sub)

        def first(rows):
            ks = [perm[self.at(r), :] for r in self.around(rows)]
            new = [harmonic(self.west(k, before), k, self.scale) for before, k in zip(ks, ks[1:-1])]
            for r, value in zip(rows, new):
                cx[self.at(r), :] = value

        self.groups(first)

        def second(rows):
            west = [cx[self.at(r), :] for r in self.around(rows)]
            found = []
            for i, r in enumerate(rows):
                k = perm[self.at(r), :]
                south = harmonic(roll(k, 2, 0), k, self.scale)
                under = jnp.where(lane < 4, 0.0, harmonic(roll(k, 4, 1), k, self.scale))
                outer = 2.0 * k * self.scale
                below = jnp.where(lane < 4, outer, under)
                above = jnp.where(lane >= 124, outer, roll(under, -4, 1))
                total = west[i + 1] + self.east(west[i + 1], west[i + 2])
                total = total + south + roll(south, -2, 0) + below + above
                found.append((south, under, total, OMEGA / total))
            for r, (south, under, total, inverse) in zip(rows, found):
                cy[self.at(r), :] = south
                cz[self.at(r), :] = under
                diag[self.at(r), :] = total
                weight[self.at(r), :] = inverse

        self.groups(second)

    def beside(self, rows, v, cx, cy, cz):
        vs = [v[self.at(r), :] for r in self.around(rows)]
        west = [cx[self.at(r), :] for r in self.around(rows)]
        flow = [c * value for c, value in zip(west[1:], vs[1:])]
        out = []
        for i, r in enumerate(rows):
            own, south, under = vs[i + 1], cy[self.at(r), :], cz[self.at(r), :]
            total = west[i + 1] * self.west(own, vs[i]) + self.east(flow[i], flow[i + 1])
            total = total + (south * roll(own, 2, 0) + roll(south * own, -2, 0))
            total = total + (under * roll(own, 4, 1) + roll(under * own, -4, 1))
            out.append((own, total))
        return out

    def start(self, v, rhs, weight):
        def body(rows):
            new = [weight[self.at(r), :] * rhs[self.at(r), :] for r in rows]
            for r, value in zip(rows, new):
                v[self.at(r), :] = value

        self.groups(body)

    def sweep(self, v, new, rhs, faces):
        cx, cy, cz, _, weight = faces

        def body(rows):
            values = [(1.0 - OMEGA) * own + weight[self.at(r), :] * (rhs[self.at(r), :] + total)
                      for r, (own, total) in zip(rows, self.beside(rows, v, cx, cy, cz))]
            for r, value in zip(rows, values):
                new[self.at(r), :] = value

        self.groups(body)

    def block_mean(self, value):
        row = row_ids(self.sub)
        value = value + jnp.where(row % 2 == 0, roll(value, -1, 0), roll(value, 1, 0))
        value = value + jnp.where(row // 2 % 2 == 0, roll(value, -2, 0), roll(value, 2, 0))
        return pair_sum(value, 4) * 0.125


class Coarsest:
    def __init__(self, rows, cols):
        self.g, self.q, self.sub = rows // 2, cols // 4, cols * 8
        self.cells = [(g, q) for g in range(self.g) for q in range(self.q)]
        self.scale = 0.25**3

    def at(self, r, c):
        return pl.ds(r * self.sub + c * 8, 8)

    def pack(self, ref):
        sublane, lane = row_ids(8) % 4, lane_ids(8) // 4 % 2
        out = {}
        for g, q in self.cells:
            halves = []
            for r in (2 * g, 2 * g + 1):
                half = ref[self.at(r, 4 * q), :]
                for c in (1, 2, 3):
                    half = jnp.where(sublane == c, ref[self.at(r, 4 * q + c), :], half)
                halves.append(half)
            out[g, q] = jnp.where(lane == 0, halves[0], halves[1])
        return out

    def repeated(self, v, r, c):
        value = v[r // 2, c // 4]
        high = lane_ids(8) // 4 % 2
        value = jnp.where(high == r % 2, value, roll(value, 4 if r % 2 == 0 else -4, 1))
        row = row_ids(8)
        value = jnp.where(row % 4 == c % 4, value, 0.0)
        value = value + jnp.where(row % 2 == 0, roll(value, -1, 0), roll(value, 1, 0))
        return value + jnp.where(row // 2 % 2 == 0, roll(value, -2, 0), roll(value, 2, 0))

    def lower_x(self, v, g, q):
        here = lane_ids(8) % 8 > 0
        return jnp.where(here, roll(v[g, q], 1, 1), roll(v[(g - 1) % self.g, q], -7, 1))

    def upper_x(self, v, g, q):
        here = lane_ids(8) % 8 < 7
        return jnp.where(here, roll(v[g, q], -1, 1), roll(v[(g + 1) % self.g, q], 7, 1))

    def lower_y(self, v, g, q):
        row = row_ids(8)
        other = jnp.where(row == 0, roll(v[g, (q - 1) % self.q], 1, 0), roll(v[g, q], -3, 0))
        return jnp.where(row >= 4, roll(v[g, q], 4, 0), other)

    def upper_y(self, v, g, q):
        row = row_ids(8)
        other = jnp.where(row == 7, roll(v[g, (q + 1) % self.q], -1, 0), roll(v[g, q], 3, 0))
        return jnp.where(row < 4, roll(v[g, q], 4, 0), other)

    def faces(self, k):
        lane = lane_ids(8)
        cx = {i: harmonic(self.lower_x(k, *i), k[i], self.scale) for i in self.cells}
        cy = {i: harmonic(self.lower_y(k, *i), k[i], self.scale) for i in self.cells}
        out = {}
        for i in self.cells:
            under = jnp.where(lane < 8, 0.0, harmonic(roll(k[i], 8, 1), k[i], self.scale))
            over = jnp.where(lane >= 120, 0.0, roll(under, -8, 1))
            outer = 2.0 * k[i] * self.scale
            below, above = jnp.where(lane < 8, outer, under), jnp.where(lane >= 120, outer, over)
            east, north = self.upper_x(cx, *i), self.upper_y(cy, *i)
            total = cx[i] + east + cy[i] + north + below + above
            weight = OMEGA / total
            out[i] = [weight * c for c in (cx[i], east, cy[i], north, under, over)] + [weight]
        return out

    def solve(self, faces, rhs):
        start = {i: faces(i, 6) * rhs[i] for i in self.cells}

        def sweep(_, carry):
            v = dict(zip(self.cells, carry))
            new = []
            for i in self.cells:
                side_x = faces(i, 0) * self.lower_x(v, *i) + faces(i, 1) * self.upper_x(v, *i)
                side_y = faces(i, 2) * self.lower_y(v, *i) + faces(i, 3) * self.upper_y(v, *i)
                side_z = faces(i, 4) * roll(v[i], 8, 1) + faces(i, 5) * roll(v[i], -8, 1)
                new.append(((1.0 - OMEGA) * v[i] + start[i] + side_z) + (side_x + side_y))
            return tuple(new)

        done = lax.fori_loop(1, CSWEEPS, sweep, tuple(start[i] for i in self.cells))
        return dict(zip(self.cells, done))


class Exchange:
    def __init__(self, win, items, bufs, sems, base, ids):
        self.win, self.items, self.ids = win, items, ids
        self.ystage, self.yland, self.cstage, self.cland = bufs
        self.sems, self.base = sems, base
        self.layers = sum(h for _, h in items)

    def remote(self, src, dst, to):
        send, recv = self.sems
        copy = pltpu.make_async_remote_copy(
            src_ref=src, dst_ref=dst, send_sem=send.at[self.base], recv_sem=recv.at[self.base],
            device_id=to, device_id_type=MESH)
        self.base += 1
        copy.start()
        return copy

    def edge(self, h, side, i):
        ny, sub = self.win.ny, self.win.sub
        return (i, ny + i) if side == 0 else (ny - h + i, sub - h + i)

    def start(self):
        (me_r, me_c), near_r, near_c = self.ids
        nx, sub = self.win.nx, self.win.sub
        self.copies = []
        for side in (0, 1):
            n = 0
            for ref, h in self.items:
                for i in range(h):
                    mine, _ = self.edge(h, side, i)
                    self.ystage[side, n:n + nx, :] = ref[pl.ds(PAD * sub + mine, nx, stride=sub), :]
                    n += nx
            to = (me_r, near_c[side])
            self.copies.append(self.remote(self.ystage.at[side], self.yland.at[side], to))
        for ref, h in self.items:
            rows = h * sub
            for side, mine, theirs in ((0, PAD, PAD + nx), (1, PAD + nx - h, PAD - h)):
                self.copies.append(self.remote(
                    ref.at[pl.ds(mine * sub, rows), :], ref.at[pl.ds(theirs * sub, rows), :],
                    (near_r[side], me_c)))
        for xside in (0, 1):
            for side in (0, 1):
                n, slot = 0, 2 * xside + side
                for ref, h in self.items:
                    first = PAD if xside == 0 else PAD + nx - h
                    for i in range(h):
                        mine, _ = self.edge(h, side, i)
                        self.cstage[slot, n:n + h, :] = ref[pl.ds(first * sub + mine, h, stride=sub), :]
                        n += h
                to = (near_r[xside], near_c[side])
                self.copies.append(self.remote(self.cstage.at[slot], self.cland.at[slot], to))

    def finish(self):
        nx, sub = self.win.nx, self.win.sub
        for copy in self.copies:
            copy.wait()
        for side in (0, 1):
            n, m = 0, 0
            for ref, h in self.items:
                for i in range(h):
                    _, halo = self.edge(h, side, i)
                    ref[pl.ds(PAD * sub + halo, nx, stride=sub), :] = self.yland[side, n:n + nx, :]
                    n += nx
                    for xside, first in ((0, PAD + nx), (1, PAD - h)):
                        corner = self.cland[2 * xside + side, m:m + h, :]
                        ref[pl.ds(first * sub + halo, h, stride=sub), :] = corner
                    m += h


def stage_sizes(win, halos):
    layers = sum(halos)
    corner = sum(h * h for h in halos)
    corner = (corner + 7) // 8 * 8
    return [(2, layers * win.nx, 128)] * 2 + [(4, corner, 128)] * 2


def wrapped(value, size):
    return jnp.where(value >= size, value - size, value)


def others(sizes, ids, body):
    rows, cols = sizes
    me_r, me_c = ids[0]
    to_cols = [me_c] + [wrapped(me_c + cols - c, cols) for c in range(1, cols)]

    def row(r, carry):
        to_row = wrapped(me_r + rows - r, rows)
        for c in range(cols):
            body(r * cols + c, (to_row, to_cols[c]))
        return carry

    for c in range(1, cols):
        body(c, (me_r, to_cols[c]))
    lax.fori_loop(1, rows, row, 0, unroll=rows <= 8)


def gather(src, land, sems, sizes, ids):
    def one(slot, to):
        at = slot * 8 if isinstance(slot, int) else pl.multiple_of(slot * 8, 8)
        pltpu.make_async_remote_copy(
            src_ref=src, dst_ref=land.at[pl.ds(at, 8), :], send_sem=sems[0], recv_sem=sems[1],
            device_id=to, device_id_type=MESH).start()

    others(sizes, ids, one)


def gather_wait(land, tiles, sems, ids):
    (me_r, me_c), (left, _), _ = ids
    span = land.at[pl.ds(8, (tiles - 1) * 8), :]
    done = pltpu.make_async_remote_copy(
        src_ref=span, dst_ref=span, send_sem=sems[0], recv_sem=sems[1],
        device_id=(left, me_c), device_id_type=MESH)
    done.wait_send()
    done.wait_recv()


def cycle_kernel(sizes, wins, p_hbm, s_hbm, k_hbm, out, *scratch):
    rows, cols = sizes
    tiles = rows * cols
    fine, mid = wins
    scratch = list(scratch)

    def take(count):
        got, scratch[:count] = scratch[:count], []
        return got

    p_in, s_in, k_in, in_sems = take(4)
    pw, pa, pb, sw, kw, vw = take(6)
    faces0 = take(5)
    b1, k1, va, vb, v1 = take(5)
    faces1 = take(5)
    k2, b2, p2a, p2b, b3 = take(5)
    faces2 = take(5)
    faces3 = take(1)[0]
    tmp, tile_b, tile_k = take(3)
    send, recv, gsend, grecv = take(4)
    bufs = [take(4) for _ in range(6)]

    loads = []
    for i, (src, dst) in enumerate(((k_hbm, k_in), (p_hbm, p_in), (s_hbm, s_in))):
        loads.append(pltpu.make_async_copy(src, dst, in_sems.at[i]))
        loads[-1].start()

    me_r, me_c = lax.axis_index("row"), lax.axis_index("col")
    ids = ((me_r, me_c),
           (wrapped(me_r + rows - 1, rows), wrapped(me_r + 1, rows)),
           (wrapped(me_c + cols - 1, cols), wrapped(me_c + 1, cols)))

    barrier = pltpu.get_barrier_semaphore()
    others(sizes, ids, lambda _, to: pl.semaphore_signal(
        barrier, inc=1, device_id=to, device_id_type=MESH))

    nx, ny, sub = fine.nx, fine.ny, fine.sub

    def bring(pairs):
        def body(i, carry):
            for x in range(4):
                at = pl.ds(pl.multiple_of((4 * i + x + PAD) * sub, 8), ny)
                for src, dst in pairs:
                    dst[at, :] = src[4 * i + x]
            return carry

        lax.fori_loop(0, nx // 4, body, 0)

    base = 0

    def exchange(win, items, buf):
        nonlocal base
        made = Exchange(win, items, buf, (send, recv), base, ids)
        made.start()
        base = made.base
        return made

    loads[0].wait()
    bring([(k_in, kw)])
    loads[1].wait()
    loads[2].wait()
    bring([(p_in, pw), (s_in, sw)])
    pl.semaphore_wait(barrier, tiles - 1)
    halo_k = exchange(fine, [(kw, 3)], bufs[0])
    halo_p = exchange(fine, [(pw, 3), (sw, 2)], bufs[1])

    def halves(slot, value, n):
        at = slot * sub
        tmp[at:at + value.shape[0], :] = value
        return lambda: tmp[pl.ds(at, n, stride=2), :] + tmp[pl.ds(at + 1, n, stride=2), :]

    def to_mid(i, ref, sums):
        made = [halves(n, value, ny // 2) for n, value in enumerate(sums)]
        made = [value() * 0.125 for value in made]
        for n, value in enumerate(made):
            at = (i * len(sums) + n + PAD) * mid.sub
            ref[pl.ds(pl.multiple_of(at, 8), mid.ny), :] = value

    def k_mean(i, carry):
        to_mid(i, k1, [pair_sum(k_in[8 * i + 2 * n] + k_in[8 * i + 2 * n + 1], 1) for n in range(4)])
        return carry

    lax.fori_loop(0, nx // 8, k_mean, 0)

    def to_tile(values, tile):
        n = mid.ny // 2
        lane = lane_ids(n)
        made = [halves(x, pair_sum(values[2 * x] + values[2 * x + 1], 2), n) for x in range(mid.nx // 2)]
        made = [value() * 0.125 for value in made]
        for i in range(2):
            pack = made[i]
            for j in range(1, 4):
                pack = jnp.where(lane % 4 == j, made[2 * j + i], pack)
            tile[pl.ds(i, n, stride=2), :] = pack

    lo, hi, lo1, hi1 = PAD, PAD + nx, PAD, PAD + mid.nx
    to_tile([k1[mid.at(x), :] for x in range(lo1, hi1)], tile_k)
    k2[0:8, :] = tile_k[...]
    gather(tile_k, k2, (gsend.at[0], grecv.at[0]), sizes, ids)
    halo_k1 = exchange(mid, [(k1, 3)], bufs[2])

    halo_k.finish()
    fine.faces(kw, *faces0, lo - 2, hi + 2, 6)
    halo_p.finish()

    def put(win, ref):
        def store(x, value):
            ref[win.at(x), :] = value
        return store

    def put_both(x, value):
        pb[fine.at(x), :] = value

    fine.sweep(pw, sw, faces0, lo - 2, hi + 2, 9, put(fine, pa))
    fine.sweep(pa, sw, faces0, lo - 1, hi + 1, 9, put_both)

    def restrict0(i, carry):
        left = fine.residual([8 * i + PAD + n for n in range(8)], pb, sw, faces0)
        to_mid(i, b1, [pair_sum(left[2 * n] + left[2 * n + 1], 1) for n in range(4)])
        return carry

    lax.fori_loop(0, nx // 8, restrict0, 0)
    halo_b1 = exchange(mid, [(b1, 2)], bufs[3])

    def keep(win, src, dst):
        def body(i, carry):
            values = [src[win.at(4 * i + n + PAD), :] for n in range(4)]
            for n in range(4):
                dst[win.at(4 * i + n + PAD), :] = values[n]
            return carry

        lax.fori_loop(0, win.nx // 4, body, 0)

    keep(fine, pb, vw)
    halo_k1.finish()
    mid.faces(k1, *faces1, lo1 - 2, hi1 + 2, 10)
    coarse2, coarse3 = Packed(rows, cols), Coarsest(rows, cols)
    halo_b1.finish()

    def zero_sweep(xs):
        new = [faces1[4][mid.at(x), :] * b1[mid.at(x), :] for x in xs]
        for x, value in zip(xs, new):
            va[mid.at(x), :] = value

    mid.groups(lo1 - 2, hi1 + 2, 10, zero_sweep)
    mid.sweep(va, b1, faces1, lo1 - 1, hi1 + 1, 11, put(mid, vb))
    to_tile(mid.residual(list(range(lo1, hi1)), vb, b1, faces1), tile_b)
    b2[0:8, :] = tile_b[...]
    gather(tile_b, b2, (gsend.at[1], grecv.at[1]), sizes, ids)
    keep(mid, vb, v1)
    halo_v1 = exchange(mid, [(v1, 3)], bufs[4])
    halo_vw = exchange(fine, [(vw, 2)], bufs[5])

    gather_wait(k2, tiles, (gsend.at[0], grecv.at[0]), ids)
    coarse2.faces(k2, *faces2)

    def k_coarsest(rs):
        new = [coarse2.block_mean(k2[coarse2.at(r), :]) for r in rs]
        for r, value in zip(rs, new):
            b3[coarse2.at(r), :] = value

    coarse2.groups(k_coarsest)
    for n, group in enumerate(coarse3.faces(coarse3.pack(b3)).values()):
        for side, value in enumerate(group):
            faces3[n, side] = value

    gather_wait(b2, tiles, (gsend.at[1], grecv.at[1]), ids)
    coarse2.start(p2a, b2, faces2[4])
    coarse2.sweep(p2a, p2b, b2, faces2)

    def restrict2(rs):
        new = [coarse2.block_mean(b2[coarse2.at(r), :] - faces2[3][coarse2.at(r), :] * own + total)
               for r, (own, total) in zip(rs, coarse2.beside(rs, p2b, *faces2[:3]))]
        for r, value in zip(rs, new):
            b3[coarse2.at(r), :] = value

    coarse2.groups(restrict2)
    e3 = coarse3.solve(lambda i, side: faces3[coarse3.cells.index(i), side], coarse3.pack(b3))
    for r in range(rows):
        for c in range(cols):
            at = coarse3.at(r, c)
            p2a[at, :] = p2b[at, :] + coarse3.repeated(e3, r, c)
    coarse2.sweep(p2a, p2b, b2, faces2)
    coarse2.sweep(p2b, p2a, b2, faces2)

    halo_v1.finish()
    span = coarse2.sub
    lane = lane_ids(span)
    places = ((-1, 3), (0, 0), (0, 1), (0, 2), (0, 3), (1, 0))
    for n, (dr, j) in enumerate(places):
        part = p2a[(dr % rows) * span:(dr % rows + 1) * span, :]
        part = pair_sum(pair_sum(jnp.where(lane % 4 == j, part, 0.0), 1), 2)
        turned = roll(part, 16 - span, 0)
        tmp[16 * n:16 * n + 16, :] = jnp.where(row_ids(16) < 12, part[0:16, :], turned[0:16, :])
    for n, (dr, j) in enumerate(places):
        for i in range(2):
            e = tmp[pl.ds(16 * n + i, 8, stride=2), :]
            x = 2 * (8 * dr + 2 * j + i) + PAD
            for row in (x, x + 1):
                for half in range(2):
                    at = pl.ds(row * mid.sub + half, 8, stride=2)
                    va[at, :] = v1[at, :] + e
    mid.sweep(va, b1, faces1, lo1 - 2, hi1 + 2, 11, put(mid, vb))
    mid.sweep(vb, b1, faces1, lo1 - 1, hi1 + 1, 11, put(mid, va))

    halo_vw.finish()

    def correct0(g, carry):
        rs = [lo1 - 1 + 6 * g + n for n in range(6)]
        for n, r in enumerate(rs):
            e = va[mid.at(r), :]
            for half in range(2):
                tmp[pl.ds(n * sub + half, 8, stride=2), :] = e[0:8, :]
                tmp[pl.ds(n * sub + 16 + half, 2, stride=2), :] = e[8:10, :]
                tmp[pl.ds(n * sub + 20 + half, 2, stride=2), :] = e[14:16, :]
        new = []
        for n, r in enumerate(rs):
            e = tmp[n * sub:(n + 1) * sub, :]
            for x in (2 * r - PAD, 2 * r - PAD + 1):
                new.append((x, vw[fine.at(x), :] + e))
        for x, value in new:
            pa[fine.at(x), :] = value
        return carry

    lax.fori_loop(0, (mid.nx + 2) // 6, correct0, 0)
    fine.sweep(pa, sw, faces0, lo - 1, hi + 1, 9, put(fine, pb))

    def give(x, value):
        out[x - PAD] = value[0:ny, :]

    fine.sweep(pb, sw, faces0, lo, hi, 8, give)


def on_device(sizes, pressure_in, source, permeability):
    rows, cols = sizes
    nx, ny, _ = pressure_in.shape
    fine, mid = Window(nx, ny, 1, 1.0), Window(nx // 2, ny // 2, 2, 0.25)

    def window(win):
        return pltpu.VMEM(((win.nx + 2 * PAD) * win.sub, 128), jnp.float32)

    packed = pltpu.VMEM((rows * cols * 8, 128), jnp.float32)
    scratch = [pltpu.VMEM(pressure_in.shape, jnp.float32)] * 3 + [pltpu.SemaphoreType.DMA((3,))]
    scratch += [window(fine)] * 11 + [window(mid)] * 10 + [packed] * 10
    scratch += [pltpu.VMEM((rows * cols // 8, 7, 8, 128), jnp.float32)]
    scratch += [pltpu.VMEM((8 * fine.sub, 128), jnp.float32)] + [pltpu.VMEM((8, 128), jnp.float32)] * 2
    scratch += [pltpu.SemaphoreType.DMA((64,))] * 2 + [pltpu.SemaphoreType.DMA((2,))] * 2
    for win, halos in ((fine, (3,)), (fine, (3, 2)), (mid, (3,)), (mid, (2,)), (mid, (3,)), (fine, (2,))):
        scratch += [pltpu.VMEM(size, jnp.float32) for size in stage_sizes(win, halos)]
    anywhere = pl.BlockSpec(memory_space=pl.ANY)
    return pl.pallas_call(
        functools.partial(cycle_kernel, sizes, (fine, mid)),
        out_shape=jax.ShapeDtypeStruct(pressure_in.shape, jnp.float32),
        in_specs=[anywhere] * 3,
        out_specs=pl.BlockSpec(memory_space=pltpu.VMEM),
        scratch_shapes=scratch,
        compiler_params=pltpu.CompilerParams(
            collective_id=0, has_side_effects=True, vmem_limit_bytes=58 * 1024 * 1024),
    )(pressure_in, source, permeability)


def solution(mesh):
    sizes = (mesh.shape["row"], mesh.shape["col"])
    placed = (P("row", "col", None), P("row", "col", None), P("row", "col", None))
    return jax.shard_map(
        functools.partial(on_device, sizes), mesh=mesh, in_specs=placed,
        out_specs=P("row", "col", None), check_vma=False)
```

```python
import functools

import jax
import jax.numpy as jnp
from jax import lax
from jax.experimental import pallas as pl
from jax.experimental.pallas import tpu as pltpu
from jax.sharding import PartitionSpec as P

MESH = pl.DeviceIdType.MESH
OMEGA = 0.8
CSWEEPS = 16
PAD = 4


def lane_ids(rows):
    return lax.broadcasted_iota(jnp.int32, (rows, 128), 1)


def row_ids(rows):
    return lax.broadcasted_iota(jnp.int32, (rows, 128), 0)


def roll(value, shift, axis):
    return pltpu.roll(value, shift % value.shape[axis], axis)


def harmonic(left, right, scale):
    return (2.0 * scale) * left * right / (left + right)


def pair_sum(value, step):
    low = (lane_ids(value.shape[0]) // step) % 2 == 0
    return value + jnp.where(low, roll(value, -step, 1), roll(value, step, 1))


class Window:
    def __init__(self, nx, ny, step, scale):
        self.nx, self.ny, self.sub, self.step, self.scale = nx, ny, ny + 2 * PAD, step, scale

    def at(self, x):
        start = x * self.sub
        if not isinstance(x, int):
            start = pl.multiple_of(start, 8)
        return pl.ds(start, self.sub)

    def groups(self, lo, hi, most, body):
        count = -(-(hi - lo) // most)
        size = -(-(hi - lo) // count)

        def step(g, carry):
            start = jnp.minimum(lo + g * size, hi - size)
            body([start + i for i in range(size)])
            return carry

        lax.fori_loop(0, count, step, 0)

    def faces(self, perm, cx, cy, cz, diag, weight, lo, hi, most):
        lane = lane_ids(self.sub)

        def body(rows):
            ks = [perm[self.at(x), :] for x in [rows[0] - 1] + rows + [rows[-1] + 1]]
            west = [harmonic(k, other, self.scale) for k, other in zip(ks[:-1], ks[1:])]
            found = []
            for i, k in enumerate(ks[1:-1]):
                south = harmonic(roll(k, 1, 0), k, self.scale)
                under = harmonic(roll(k, self.step, 1), k, self.scale)
                under = jnp.where(lane < self.step, 0.0, under)
                outer = 2.0 * k * self.scale
                below = jnp.where(lane < self.step, outer, under)
                above = jnp.where(lane >= 128 - self.step, outer, roll(under, -self.step, 1))
                total = west[i] + west[i + 1] + south + roll(south, -1, 0) + below + above
                found.append((south, under, total, OMEGA / total))
            for x, lower, (south, under, total, inverse) in zip(rows, west, found):
                cx[self.at(x), :] = lower
                cy[self.at(x), :] = south
                cz[self.at(x), :] = under
                diag[self.at(x), :] = total
                weight[self.at(x), :] = inverse
            cx[self.at(rows[-1] + 1), :] = west[-1]

        self.groups(lo, hi, most, body)

    def beside(self, rows, v, cx, cy, cz):
        vs = [v[self.at(x), :] for x in [rows[0] - 1] + rows + [rows[-1] + 1]]
        west = [cx[self.at(x), :] for x in rows + [rows[-1] + 1]]
        out = []
        for i, x in enumerate(rows):
            own, south, under = vs[i + 1], cy[self.at(x), :], cz[self.at(x), :]
            total = west[i] * vs[i] + west[i + 1] * vs[i + 2]
            total = total + (south * roll(own, 1, 0) + roll(south * own, -1, 0))
            total = total + (under * roll(own, self.step, 1) + roll(under * own, -self.step, 1))
            out.append((own, total))
        return out

    def sweep(self, v, rhs, faces, lo, hi, most, store):
        cx, cy, cz, _, weight = faces

        def body(rows):
            new = [(1.0 - OMEGA) * own + weight[self.at(x), :] * (rhs[self.at(x), :] + total)
                   for x, (own, total) in zip(rows, self.beside(rows, v, cx, cy, cz))]
            for x, value in zip(rows, new):
                store(x, value)

        self.groups(lo, hi, most, body)

    def residual(self, rows, v, rhs, faces):
        cx, cy, cz, diag, _ = faces
        return [rhs[self.at(x), :] - diag[self.at(x), :] * own + total
                for x, (own, total) in zip(rows, self.beside(rows, v, cx, cy, cz))]


class Packed:
    def __init__(self, rows, cols):
        self.rows, self.cols, self.sub = rows, cols, cols * 8
        self.scale = 0.25**2

    def at(self, r):
        return pl.ds(pl.multiple_of(r * self.sub, 8), self.sub)

    def west(self, here, before):
        j = lane_ids(self.sub) % 4
        odd = row_ids(self.sub) % 2 == 1
        up, up_before = roll(here, -1, 0), roll(before, -1, 0)
        other = jnp.where(j > 0, roll(up, 1, 1), roll(up_before, -3, 1))
        return jnp.where(odd, roll(here, 1, 0), other)

    def east(self, here, after):
        j = lane_ids(self.sub) % 4
        odd = row_ids(self.sub) % 2 == 1
        down, down_after = roll(here, 1, 0), roll(after, 1, 0)
        other = jnp.where(j < 3, roll(down, -1, 1), roll(down_after, 3, 1))
        return jnp.where(odd, other, roll(here, -1, 0))

    def groups(self, body):
        size = 4 if self.rows % 4 == 0 else 1

        def step(g, carry):
            body([g * size + i for i in range(size)])
            return carry

        lax.fori_loop(0, self.rows // size, step, 0)

    def around(self, rows):
        return [lax.rem(rows[0] + self.rows - 1, self.rows)] + rows + [lax.rem(rows[-1] + 1, self.rows)]

    def faces(self, perm, cx, cy, cz, diag, weight):
        lane = lane_ids(self.sub)

        def first(rows):
            ks = [perm[self.at(r), :] for r in self.around(rows)]
            new = [harmonic(self.west(k, before), k, self.scale) for before, k in zip(ks, ks[1:-1])]
            for r, value in zip(rows, new):
                cx[self.at(r), :] = value

        self.groups(first)

        def second(rows):
            west = [cx[self.at(r), :] for r in self.around(rows)]
            found = []
            for i, r in enumerate(rows):
                k = perm[self.at(r), :]
                south = harmonic(roll(k, 2, 0), k, self.scale)
                under = jnp.where(lane < 4, 0.0, harmonic(roll(k, 4, 1), k, self.scale))
                outer = 2.0 * k * self.scale
                below = jnp.where(lane < 4, outer, under)
                above = jnp.where(lane >= 124, outer, roll(under, -4, 1))
                total = west[i + 1] + self.east(west[i + 1], west[i + 2])
                total = total + south + roll(south, -2, 0) + below + above
                found.append((south, under, total, OMEGA / total))
            for r, (south, under, total, inverse) in zip(rows, found):
                cy[self.at(r), :] = south
                cz[self.at(r), :] = under
                diag[self.at(r), :] = total
                weight[self.at(r), :] = inverse

        self.groups(second)

    def beside(self, rows, v, cx, cy, cz):
        vs = [v[self.at(r), :] for r in self.around(rows)]
        west = [cx[self.at(r), :] for r in self.around(rows)]
        flow = [c * value for c, value in zip(west[1:], vs[1:])]
        out = []
        for i, r in enumerate(rows):
            own, south, under = vs[i + 1], cy[self.at(r), :], cz[self.at(r), :]
            total = west[i + 1] * self.west(own, vs[i]) + self.east(flow[i], flow[i + 1])
            total = total + (south * roll(own, 2, 0) + roll(south * own, -2, 0))
            total = total + (under * roll(own, 4, 1) + roll(under * own, -4, 1))
            out.append((own, total))
        return out

    def start(self, v, rhs, weight):
        def body(rows):
            new = [weight[self.at(r), :] * rhs[self.at(r), :] for r in rows]
            for r, value in zip(rows, new):
                v[self.at(r), :] = value

        self.groups(body)

    def sweep(self, v, new, rhs, faces):
        cx, cy, cz, _, weight = faces

        def body(rows):
            values = [(1.0 - OMEGA) * own + weight[self.at(r), :] * (rhs[self.at(r), :] + total)
                      for r, (own, total) in zip(rows, self.beside(rows, v, cx, cy, cz))]
            for r, value in zip(rows, values):
                new[self.at(r), :] = value

        self.groups(body)

    def block_mean(self, value):
        row = row_ids(self.sub)
        value = value + jnp.where(row % 2 == 0, roll(value, -1, 0), roll(value, 1, 0))
        value = value + jnp.where(row // 2 % 2 == 0, roll(value, -2, 0), roll(value, 2, 0))
        return pair_sum(value, 4) * 0.125


class Coarsest:
    def __init__(self, rows, cols):
        self.g, self.q, self.sub = rows // 2, cols // 4, cols * 8
        self.cells = [(g, q) for g in range(self.g) for q in range(self.q)]
        self.scale = 0.25**3

    def at(self, r, c):
        return pl.ds(r * self.sub + c * 8, 8)

    def pack(self, ref):
        sublane, lane = row_ids(8) % 4, lane_ids(8) // 4 % 2
        out = {}
        for g, q in self.cells:
            halves = []
            for r in (2 * g, 2 * g + 1):
                half = ref[self.at(r, 4 * q), :]
                for c in (1, 2, 3):
                    half = jnp.where(sublane == c, ref[self.at(r, 4 * q + c), :], half)
                halves.append(half)
            out[g, q] = jnp.where(lane == 0, halves[0], halves[1])
        return out

    def repeated(self, v, r, c):
        value = v[r // 2, c // 4]
        high = lane_ids(8) // 4 % 2
        value = jnp.where(high == r % 2, value, roll(value, 4 if r % 2 == 0 else -4, 1))
        row = row_ids(8)
        value = jnp.where(row % 4 == c % 4, value, 0.0)
        value = value + jnp.where(row % 2 == 0, roll(value, -1, 0), roll(value, 1, 0))
        return value + jnp.where(row // 2 % 2 == 0, roll(value, -2, 0), roll(value, 2, 0))

    def lower_x(self, v, g, q):
        here = lane_ids(8) % 8 > 0
        return jnp.where(here, roll(v[g, q], 1, 1), roll(v[(g - 1) % self.g, q], -7, 1))

    def upper_x(self, v, g, q):
        here = lane_ids(8) % 8 < 7
        return jnp.where(here, roll(v[g, q], -1, 1), roll(v[(g + 1) % self.g, q], 7, 1))

    def lower_y(self, v, g, q):
        row = row_ids(8)
        other = jnp.where(row == 0, roll(v[g, (q - 1) % self.q], 1, 0), roll(v[g, q], -3, 0))
        return jnp.where(row >= 4, roll(v[g, q], 4, 0), other)

    def upper_y(self, v, g, q):
        row = row_ids(8)
        other = jnp.where(row == 7, roll(v[g, (q + 1) % self.q], -1, 0), roll(v[g, q], 3, 0))
        return jnp.where(row < 4, roll(v[g, q], 4, 0), other)

    def faces(self, k):
        lane = lane_ids(8)
        cx = {i: harmonic(self.lower_x(k, *i), k[i], self.scale) for i in self.cells}
        cy = {i: harmonic(self.lower_y(k, *i), k[i], self.scale) for i in self.cells}
        out = {}
        for i in self.cells:
            under = jnp.where(lane < 8, 0.0, harmonic(roll(k[i], 8, 1), k[i], self.scale))
            over = jnp.where(lane >= 120, 0.0, roll(under, -8, 1))
            outer = 2.0 * k[i] * self.scale
            below, above = jnp.where(lane < 8, outer, under), jnp.where(lane >= 120, outer, over)
            east, north = self.upper_x(cx, *i), self.upper_y(cy, *i)
            total = cx[i] + east + cy[i] + north + below + above
            weight = OMEGA / total
            out[i] = [weight * c for c in (cx[i], east, cy[i], north, under, over)] + [weight]
        return out

    def solve(self, faces, rhs):
        start = {i: faces(i, 6) * rhs[i] for i in self.cells}

        def sweep(_, carry):
            v = dict(zip(self.cells, carry))
            new = []
            for i in self.cells:
                side_x = faces(i, 0) * self.lower_x(v, *i) + faces(i, 1) * self.upper_x(v, *i)
                side_y = faces(i, 2) * self.lower_y(v, *i) + faces(i, 3) * self.upper_y(v, *i)
                side_z = faces(i, 4) * roll(v[i], 8, 1) + faces(i, 5) * roll(v[i], -8, 1)
                new.append(((1.0 - OMEGA) * v[i] + start[i] + side_z) + (side_x + side_y))
            return tuple(new)

        done = lax.fori_loop(1, CSWEEPS, sweep, tuple(start[i] for i in self.cells))
        return dict(zip(self.cells, done))


class Exchange:
    def __init__(self, win, items, bufs, sems, base, ids):
        self.win, self.items, self.ids = win, items, ids
        self.ystage, self.yland, self.cstage, self.cland = bufs
        self.sems, self.base = sems, base
        self.layers = sum(h for _, h in items)

    def remote(self, src, dst, to):
        send, recv = self.sems
        copy = pltpu.make_async_remote_copy(
            src_ref=src, dst_ref=dst, send_sem=send.at[self.base], recv_sem=recv.at[self.base],
            device_id=to, device_id_type=MESH)
        self.base += 1
        copy.start()
        return copy

    def edge(self, h, side, i):
        ny, sub = self.win.ny, self.win.sub
        return (i, ny + i) if side == 0 else (ny - h + i, sub - h + i)

    def start(self):
        (me_r, me_c), near_r, near_c = self.ids
        nx, sub = self.win.nx, self.win.sub
        self.copies = []
        for side in (0, 1):
            n = 0
            for ref, h in self.items:
                for i in range(h):
                    mine, _ = self.edge(h, side, i)
                    self.ystage[side, n:n + nx, :] = ref[pl.ds(PAD * sub + mine, nx, stride=sub), :]
                    n += nx
            to = (me_r, near_c[side])
            self.copies.append(self.remote(self.ystage.at[side], self.yland.at[side], to))
        for ref, h in self.items:
            rows = h * sub
            for side, mine, theirs in ((0, PAD, PAD + nx), (1, PAD + nx - h, PAD - h)):
                self.copies.append(self.remote(
                    ref.at[pl.ds(mine * sub, rows), :], ref.at[pl.ds(theirs * sub, rows), :],
                    (near_r[side], me_c)))
        for xside in (0, 1):
            for side in (0, 1):
                n, slot = 0, 2 * xside + side
                for ref, h in self.items:
                    first = PAD if xside == 0 else PAD + nx - h
                    for i in range(h):
                        mine, _ = self.edge(h, side, i)
                        self.cstage[slot, n:n + h, :] = ref[pl.ds(first * sub + mine, h, stride=sub), :]
                        n += h
                to = (near_r[xside], near_c[side])
                self.copies.append(self.remote(self.cstage.at[slot], self.cland.at[slot], to))

    def finish(self):
        nx, sub = self.win.nx, self.win.sub
        for copy in self.copies:
            copy.wait()
        for side in (0, 1):
            n, m = 0, 0
            for ref, h in self.items:
                for i in range(h):
                    _, halo = self.edge(h, side, i)
                    ref[pl.ds(PAD * sub + halo, nx, stride=sub), :] = self.yland[side, n:n + nx, :]
                    n += nx
                    for xside, first in ((0, PAD + nx), (1, PAD - h)):
                        corner = self.cland[2 * xside + side, m:m + h, :]
                        ref[pl.ds(first * sub + halo, h, stride=sub), :] = corner
                    m += h


def stage_sizes(win, halos):
    layers = sum(halos)
    corner = sum(h * h for h in halos)
    corner = (corner + 7) // 8 * 8
    return [(2, layers * win.nx, 128)] * 2 + [(4, corner, 128)] * 2


def wrapped(value, size):
    return jnp.where(value >= size, value - size, value)


def others(sizes, ids, body):
    rows, cols = sizes
    me_r, me_c = ids[0]
    to_cols = [me_c] + [wrapped(me_c + cols - c, cols) for c in range(1, cols)]

    def row(r, carry):
        to_row = wrapped(me_r + rows - r, rows)
        for c in range(cols):
            body(r * cols + c, (to_row, to_cols[c]))
        return carry

    for c in range(1, cols):
        body(c, (me_r, to_cols[c]))
    lax.fori_loop(1, rows, row, 0, unroll=rows <= 8)


def gather(src, land, sems, sizes, ids):
    def one(slot, to):
        at = slot * 8 if isinstance(slot, int) else pl.multiple_of(slot * 8, 8)
        pltpu.make_async_remote_copy(
            src_ref=src, dst_ref=land.at[pl.ds(at, 8), :], send_sem=sems[0], recv_sem=sems[1],
            device_id=to, device_id_type=MESH).start()

    others(sizes, ids, one)


def gather_wait(land, tiles, sems, ids):
    (me_r, me_c), (left, _), _ = ids
    span = land.at[pl.ds(8, (tiles - 1) * 8), :]
    done = pltpu.make_async_remote_copy(
        src_ref=span, dst_ref=span, send_sem=sems[0], recv_sem=sems[1],
        device_id=(left, me_c), device_id_type=MESH)
    done.wait_send()
    done.wait_recv()


def cycle_kernel(sizes, wins, p_hbm, s_hbm, k_hbm, out, *scratch):
    rows, cols = sizes
    tiles = rows * cols
    fine, mid = wins
    scratch = list(scratch)

    def take(count):
        got, scratch[:count] = scratch[:count], []
        return got

    p_in, s_in, k_in, in_sems = take(4)
    pw, pa, pb, sw, kw, vw = take(6)
    faces0 = take(5)
    b1, k1, va, vb, v1 = take(5)
    faces1 = take(5)
    k2, b2, p2a, p2b, b3 = take(5)
    faces2 = take(5)
    faces3 = take(1)[0]
    tmp, tile_b, tile_k = take(3)
    send, recv, gsend, grecv = take(4)
    bufs = [take(4) for _ in range(6)]

    loads = []
    for i, (src, dst) in enumerate(((k_hbm, k_in), (p_hbm, p_in), (s_hbm, s_in))):
        loads.append(pltpu.make_async_copy(src, dst, in_sems.at[i]))
        loads[-1].start()

    me_r, me_c = lax.axis_index("row"), lax.axis_index("col")
    ids = ((me_r, me_c),
           (wrapped(me_r + rows - 1, rows), wrapped(me_r + 1, rows)),
           (wrapped(me_c + cols - 1, cols), wrapped(me_c + 1, cols)))

    barrier = pltpu.get_barrier_semaphore()
    others(sizes, ids, lambda _, to: pl.semaphore_signal(
        barrier, inc=1, device_id=to, device_id_type=MESH))

    nx, ny, sub = fine.nx, fine.ny, fine.sub

    def bring(pairs):
        def body(i, carry):
            for x in range(4):
                at = pl.ds(pl.multiple_of((4 * i + x + PAD) * sub, 8), ny)
                for src, dst in pairs:
                    dst[at, :] = src[4 * i + x]
            return carry

        lax.fori_loop(0, nx // 4, body, 0)

    base = 0

    def exchange(win, items, buf):
        nonlocal base
        made = Exchange(win, items, buf, (send, recv), base, ids)
        made.start()
        base = made.base
        return made

    loads[0].wait()
    bring([(k_in, kw)])
    def halves(slot, value, n):
        at = slot * sub
        tmp[at:at + value.shape[0], :] = value
        return lambda: tmp[pl.ds(at, n, stride=2), :] + tmp[pl.ds(at + 1, n, stride=2), :]

    def to_mid(i, ref, sums):
        made = [halves(n, value, ny // 2) for n, value in enumerate(sums)]
        made = [value() * 0.125 for value in made]
        for n, value in enumerate(made):
            at = (i * len(sums) + n + PAD) * mid.sub
            ref[pl.ds(pl.multiple_of(at, 8), mid.ny), :] = value

    def k_mean(i, carry):
        to_mid(i, k1, [pair_sum(k_in[8 * i + 2 * n] + k_in[8 * i + 2 * n + 1], 1) for n in range(4)])
        return carry

    lax.fori_loop(0, nx // 8, k_mean, 0)

    def to_tile(values, tile):
        n = mid.ny // 2
        lane = lane_ids(n)
        made = [halves(x, pair_sum(values[2 * x] + values[2 * x + 1], 2), n) for x in range(mid.nx // 2)]
        made = [value() * 0.125 for value in made]
        for i in range(2):
            pack = made[i]
            for j in range(1, 4):
                pack = jnp.where(lane % 4 == j, made[2 * j + i], pack)
            tile[pl.ds(i, n, stride=2), :] = pack

    lo, hi, lo1, hi1 = PAD, PAD + nx, PAD, PAD + mid.nx
    to_tile([k1[mid.at(x), :] for x in range(lo1, hi1)], tile_k)
    k2[0:8, :] = tile_k[...]
    loads[1].wait()
    loads[2].wait()
    bring([(p_in, pw), (s_in, sw)])
    pl.semaphore_wait(barrier, tiles - 1)
    halo_k = exchange(fine, [(kw, 3)], bufs[0])
    halo_p = exchange(fine, [(pw, 3), (sw, 2)], bufs[1])
    halo_k.finish()
    fine.faces(kw, *faces0, lo - 2, hi + 2, 6)
    halo_p.finish()
    halo_k1 = exchange(mid, [(k1, 3)], bufs[2])
    gather(tile_k, k2, (gsend.at[0], grecv.at[0]), sizes, ids)

    def put(win, ref):
        def store(x, value):
            ref[win.at(x), :] = value
        return store

    def put_both(x, value):
        pb[fine.at(x), :] = value

    fine.sweep(pw, sw, faces0, lo - 2, hi + 2, 9, put(fine, pa))
    fine.sweep(pa, sw, faces0, lo - 1, hi + 1, 9, put_both)

    def restrict0(i, carry):
        left = fine.residual([8 * i + PAD + n for n in range(8)], pb, sw, faces0)
        to_mid(i, b1, [pair_sum(left[2 * n] + left[2 * n + 1], 1) for n in range(4)])
        return carry

    lax.fori_loop(0, nx // 8, restrict0, 0)
    halo_b1 = exchange(mid, [(b1, 2)], bufs[3])

    def keep(win, src, dst):
        def body(i, carry):
            values = [src[win.at(4 * i + n + PAD), :] for n in range(4)]
            for n in range(4):
                dst[win.at(4 * i + n + PAD), :] = values[n]
            return carry

        lax.fori_loop(0, win.nx // 4, body, 0)

    keep(fine, pb, vw)
    halo_k1.finish()
    mid.faces(k1, *faces1, lo1 - 2, hi1 + 2, 10)
    coarse2, coarse3 = Packed(rows, cols), Coarsest(rows, cols)
    halo_b1.finish()

    def zero_sweep(xs):
        new = [faces1[4][mid.at(x), :] * b1[mid.at(x), :] for x in xs]
        for x, value in zip(xs, new):
            va[mid.at(x), :] = value

    mid.groups(lo1 - 2, hi1 + 2, 10, zero_sweep)
    mid.sweep(va, b1, faces1, lo1 - 1, hi1 + 1, 11, put(mid, vb))
    to_tile(mid.residual(list(range(lo1, hi1)), vb, b1, faces1), tile_b)
    b2[0:8, :] = tile_b[...]
    gather(tile_b, b2, (gsend.at[1], grecv.at[1]), sizes, ids)
    keep(mid, vb, v1)

    gather_wait(k2, tiles, (gsend.at[0], grecv.at[0]), ids)
    coarse2.faces(k2, *faces2)

    def k_coarsest(rs):
        new = [coarse2.block_mean(k2[coarse2.at(r), :]) for r in rs]
        for r, value in zip(rs, new):
            b3[coarse2.at(r), :] = value

    coarse2.groups(k_coarsest)
    for n, group in enumerate(coarse3.faces(coarse3.pack(b3)).values()):
        for side, value in enumerate(group):
            faces3[n, side] = value

    gather_wait(b2, tiles, (gsend.at[1], grecv.at[1]), ids)
    halo_v1 = exchange(mid, [(v1, 3)], bufs[4])
    halo_vw = exchange(fine, [(vw, 2)], bufs[5])
    coarse2.start(p2a, b2, faces2[4])
    coarse2.sweep(p2a, p2b, b2, faces2)

    def restrict2(rs):
        new = [coarse2.block_mean(b2[coarse2.at(r), :] - faces2[3][coarse2.at(r), :] * own + total)
               for r, (own, total) in zip(rs, coarse2.beside(rs, p2b, *faces2[:3]))]
        for r, value in zip(rs, new):
            b3[coarse2.at(r), :] = value

    coarse2.groups(restrict2)
    e3 = coarse3.solve(lambda i, side: faces3[coarse3.cells.index(i), side], coarse3.pack(b3))
    for r in range(rows):
        for c in range(cols):
            at = coarse3.at(r, c)
            p2a[at, :] = p2b[at, :] + coarse3.repeated(e3, r, c)
    coarse2.sweep(p2a, p2b, b2, faces2)
    coarse2.sweep(p2b, p2a, b2, faces2)

    halo_v1.finish()
    span = coarse2.sub
    lane = lane_ids(span)
    places = ((-1, 3), (0, 0), (0, 1), (0, 2), (0, 3), (1, 0))
    for n, (dr, j) in enumerate(places):
        part = p2a[(dr % rows) * span:(dr % rows + 1) * span, :]
        part = pair_sum(pair_sum(jnp.where(lane % 4 == j, part, 0.0), 1), 2)
        turned = roll(part, 16 - span, 0)
        tmp[16 * n:16 * n + 16, :] = jnp.where(row_ids(16) < 12, part[0:16, :], turned[0:16, :])
    for n, (dr, j) in enumerate(places):
        for i in range(2):
            e = tmp[pl.ds(16 * n + i, 8, stride=2), :]
            x = 2 * (8 * dr + 2 * j + i) + PAD
            for row in (x, x + 1):
                for half in range(2):
                    at = pl.ds(row * mid.sub + half, 8, stride=2)
                    va[at, :] = v1[at, :] + e
    mid.sweep(va, b1, faces1, lo1 - 2, hi1 + 2, 11, put(mid, vb))
    mid.sweep(vb, b1, faces1, lo1 - 1, hi1 + 1, 11, put(mid, va))

    halo_vw.finish()

    def correct0(g, carry):
        rs = [lo1 - 1 + 6 * g + n for n in range(6)]
        for n, r in enumerate(rs):
            e = va[mid.at(r), :]
            for half in range(2):
                tmp[pl.ds(n * sub + half, 8, stride=2), :] = e[0:8, :]
                tmp[pl.ds(n * sub + 16 + half, 2, stride=2), :] = e[8:10, :]
                tmp[pl.ds(n * sub + 20 + half, 2, stride=2), :] = e[14:16, :]
        new = []
        for n, r in enumerate(rs):
            e = tmp[n * sub:(n + 1) * sub, :]
            for x in (2 * r - PAD, 2 * r - PAD + 1):
                new.append((x, vw[fine.at(x), :] + e))
        for x, value in new:
            pa[fine.at(x), :] = value
        return carry

    lax.fori_loop(0, (mid.nx + 2) // 6, correct0, 0)
    fine.sweep(pa, sw, faces0, lo - 1, hi + 1, 9, put(fine, pb))

    def last(xs):
        rest = (1.0 - OMEGA) / OMEGA
        new = [rest * own + (sw[fine.at(x), :] + total) / faces0[3][fine.at(x), :]
               for x, (own, total) in zip(xs, fine.beside(xs, pb, *faces0[:3]))]
        for x, value in zip(xs, new):
            out[x - PAD] = value[0:ny, :]

    fine.groups(lo, hi, 8, last)


def on_device(sizes, pressure_in, source, permeability):
    rows, cols = sizes
    nx, ny, _ = pressure_in.shape
    fine, mid = Window(nx, ny, 1, 1.0), Window(nx // 2, ny // 2, 2, 0.25)

    def window(win):
        return pltpu.VMEM(((win.nx + 2 * PAD) * win.sub, 128), jnp.float32)

    packed = pltpu.VMEM((rows * cols * 8, 128), jnp.float32)
    scratch = [pltpu.VMEM(pressure_in.shape, jnp.float32)] * 3 + [pltpu.SemaphoreType.DMA((3,))]
    scratch += [window(fine)] * 11 + [window(mid)] * 10 + [packed] * 10
    scratch += [pltpu.VMEM((rows * cols // 8, 7, 8, 128), jnp.float32)]
    scratch += [pltpu.VMEM((8 * fine.sub, 128), jnp.float32)] + [pltpu.VMEM((8, 128), jnp.float32)] * 2
    scratch += [pltpu.SemaphoreType.DMA((64,))] * 2 + [pltpu.SemaphoreType.DMA((2,))] * 2
    for win, halos in ((fine, (3,)), (fine, (3, 2)), (mid, (3,)), (mid, (2,)), (mid, (3,)), (fine, (2,))):
        scratch += [pltpu.VMEM(size, jnp.float32) for size in stage_sizes(win, halos)]
    anywhere = pl.BlockSpec(memory_space=pl.ANY)
    scaled = pl.pallas_call(
        functools.partial(cycle_kernel, sizes, (fine, mid)),
        out_shape=jax.ShapeDtypeStruct(pressure_in.shape, jnp.float32),
        in_specs=[anywhere] * 3,
        out_specs=pl.BlockSpec(memory_space=pltpu.VMEM),
        scratch_shapes=scratch,
        compiler_params=pltpu.CompilerParams(
            collective_id=0, has_side_effects=True, vmem_limit_bytes=58 * 1024 * 1024),
    )(pressure_in, source, permeability)
    return OMEGA * scaled


def solution(mesh):
    sizes = (mesh.shape["row"], mesh.shape["col"])
    placed = (P("row", "col", None), P("row", "col", None), P("row", "col", None))
    return jax.shard_map(
        functools.partial(on_device, sizes), mesh=mesh, in_specs=placed,
        out_specs=P("row", "col", None), check_vma=False)
```

```python
import functools

import jax
import jax.numpy as jnp
from jax import lax
from jax.experimental import pallas as pl
from jax.experimental.pallas import tpu as pltpu
from jax.sharding import PartitionSpec as P

MESH = pl.DeviceIdType.MESH
OMEGA = 0.8
CSWEEPS = 16
PAD = 4


def lane_ids(rows):
    return lax.broadcasted_iota(jnp.int32, (rows, 128), 1)


def row_ids(rows):
    return lax.broadcasted_iota(jnp.int32, (rows, 128), 0)


def roll(value, shift, axis):
    return pltpu.roll(value, shift % value.shape[axis], axis)


def harmonic(left, right, scale):
    return (2.0 * scale) * left * right / (left + right)


def pair_sum(value, step):
    low = (lane_ids(value.shape[0]) // step) % 2 == 0
    return value + jnp.where(low, roll(value, -step, 1), roll(value, step, 1))


class Window:
    def __init__(self, nx, ny, step, scale):
        self.nx, self.ny, self.sub, self.step, self.scale = nx, ny, ny + 2 * PAD, step, scale

    def at(self, x):
        start = x * self.sub
        if not isinstance(x, int):
            start = pl.multiple_of(start, 8)
        return pl.ds(start, self.sub)

    def groups(self, lo, hi, most, body):
        count = -(-(hi - lo) // most)
        size = -(-(hi - lo) // count)

        def step(g, carry):
            start = jnp.minimum(lo + g * size, hi - size)
            body([start + i for i in range(size)])
            return carry

        lax.fori_loop(0, count, step, 0)

    def faces(self, perm, cx, cy, cz, diag, weight, lo, hi, most):
        lane = lane_ids(self.sub)

        def body(rows):
            ks = [perm[self.at(x), :] for x in [rows[0] - 1] + rows + [rows[-1] + 1]]
            west = [harmonic(k, other, self.scale) for k, other in zip(ks[:-1], ks[1:])]
            found = []
            for i, k in enumerate(ks[1:-1]):
                south = harmonic(roll(k, 1, 0), k, self.scale)
                under = harmonic(roll(k, self.step, 1), k, self.scale)
                under = jnp.where(lane < self.step, 0.0, under)
                outer = 2.0 * k * self.scale
                below = jnp.where(lane < self.step, outer, under)
                above = jnp.where(lane >= 128 - self.step, outer, roll(under, -self.step, 1))
                total = west[i] + west[i + 1] + south + roll(south, -1, 0) + below + above
                found.append((south, under, total, OMEGA / total))
            for x, lower, (south, under, total, inverse) in zip(rows, west, found):
                cx[self.at(x), :] = lower
                cy[self.at(x), :] = south
                cz[self.at(x), :] = under
                diag[self.at(x), :] = total
                weight[self.at(x), :] = inverse
            cx[self.at(rows[-1] + 1), :] = west[-1]

        self.groups(lo, hi, most, body)

    def beside(self, rows, v, cx, cy, cz):
        vs = [v[self.at(x), :] for x in [rows[0] - 1] + rows + [rows[-1] + 1]]
        west = [cx[self.at(x), :] for x in rows + [rows[-1] + 1]]
        out = []
        for i, x in enumerate(rows):
            own, south, under = vs[i + 1], cy[self.at(x), :], cz[self.at(x), :]
            total = west[i] * vs[i] + west[i + 1] * vs[i + 2]
            total = total + (south * roll(own, 1, 0) + roll(south * own, -1, 0))
            total = total + (under * roll(own, self.step, 1) + roll(under * own, -self.step, 1))
            out.append((own, total))
        return out

    def sweep(self, v, rhs, faces, lo, hi, most, store):
        cx, cy, cz, _, weight = faces

        def body(rows):
            new = [(1.0 - OMEGA) * own + weight[self.at(x), :] * (rhs[self.at(x), :] + total)
                   for x, (own, total) in zip(rows, self.beside(rows, v, cx, cy, cz))]
            for x, value in zip(rows, new):
                store(x, value)

        self.groups(lo, hi, most, body)

    def residual(self, rows, v, rhs, faces):
        cx, cy, cz, diag, _ = faces
        return [rhs[self.at(x), :] - diag[self.at(x), :] * own + total
                for x, (own, total) in zip(rows, self.beside(rows, v, cx, cy, cz))]


class Packed:
    def __init__(self, rows, cols):
        self.rows, self.cols, self.sub = rows, cols, cols * 4
        self.scale = 0.25**2

    def at(self, r):
        start = r * self.sub
        return pl.ds(start if isinstance(r, int) else pl.multiple_of(start, 8), self.sub)

    def landed(self, ref, r):
        start = pl.multiple_of(r * self.sub * 2, 8)
        return [ref[pl.ds(start + i, self.sub, stride=2), :] for i in range(2)]

    def load(self, ref, r):
        return [ref[i, self.at(r), :] for i in range(2)]

    def save(self, ref, r, pair):
        for i in range(2):
            ref[i, self.at(r), :] = pair[i]

    def west(self, before, here):
        j = lane_ids(self.sub) % 4
        return [jnp.where(j > 0, roll(here[1], 1, 1), roll(before[1], -3, 1)), here[0]]

    def east(self, here, after):
        j = lane_ids(self.sub) % 4
        return [here[1], jnp.where(j < 3, roll(here[0], -1, 1), roll(after[0], 3, 1))]

    def groups(self, body):
        size = 4 if self.rows % 4 == 0 else 1

        def step(g, carry):
            body([g * size + i for i in range(size)])
            return carry

        lax.fori_loop(0, self.rows // size, step, 0)

    def around(self, rows):
        return [lax.rem(rows[0] + self.rows - 1, self.rows)] + rows + [lax.rem(rows[-1] + 1, self.rows)]

    def faces(self, landed, cx, cy, cz, diag, weight):
        lane = lane_ids(self.sub)

        def first(rows):
            ks = [self.landed(landed, r) for r in self.around(rows)]
            new = [[harmonic(w, k, self.scale) for w, k in zip(self.west(before, here), here)]
                   for before, here in zip(ks, ks[1:-1])]
            for r, pair in zip(rows, new):
                self.save(cx, r, pair)

        self.groups(first)

        def second(rows):
            west = [self.load(cx, r) for r in self.around(rows)]
            found = []
            for n, r in enumerate(rows):
                east = self.east(west[n + 1], west[n + 2])
                both = []
                for i, k in enumerate(self.landed(landed, r)):
                    south = harmonic(roll(k, 1, 0), k, self.scale)
                    under = jnp.where(lane < 4, 0.0, harmonic(roll(k, 4, 1), k, self.scale))
                    outer = 2.0 * k * self.scale
                    below = jnp.where(lane < 4, outer, under)
                    above = jnp.where(lane >= 124, outer, roll(under, -4, 1))
                    total = west[n + 1][i] + east[i] + south + roll(south, -1, 0) + below + above
                    both.append((south, under, total, OMEGA / total))
                found.append(list(zip(*both)))
            for r, values in zip(rows, found):
                for ref, pair in zip((cy, cz, diag, weight), values):
                    self.save(ref, r, pair)

        self.groups(second)

    def beside(self, rows, v, cx, cy, cz):
        vs = [self.load(v, r) for r in self.around(rows)]
        west = [self.load(cx, r) for r in self.around(rows)]
        flow = [[c * value for c, value in zip(cs, both)] for cs, both in zip(west, vs)]
        out = []
        for n, r in enumerate(rows):
            lower, upper = self.west(vs[n], vs[n + 1]), self.east(flow[n + 1], flow[n + 2])
            souths, unders, pair = self.load(cy, r), self.load(cz, r), []
            for i in range(2):
                own, south, under = vs[n + 1][i], souths[i], unders[i]
                total = west[n + 1][i] * lower[i] + upper[i]
                total = total + (south * roll(own, 1, 0) + roll(south * own, -1, 0))
                total = total + (under * roll(own, 4, 1) + roll(under * own, -4, 1))
                pair.append((own, total))
            out.append(pair)
        return out

    def start(self, v, rhs, weight):
        def body(rows):
            new = [[w * b for w, b in zip(self.load(weight, r), self.landed(rhs, r))] for r in rows]
            for r, pair in zip(rows, new):
                self.save(v, r, pair)

        self.groups(body)

    def sweep(self, v, new, rhs, faces):
        cx, cy, cz, _, weight = faces

        def body(rows):
            values = []
            for r, found in zip(rows, self.beside(rows, v, cx, cy, cz)):
                parts = zip(found, self.load(weight, r), self.landed(rhs, r))
                values.append([(1.0 - OMEGA) * own + w * (b + total) for (own, total), w, b in parts])
            for r, pair in zip(rows, values):
                self.save(new, r, pair)

        self.groups(body)

    def block_mean(self, pair):
        value = pair[0] + pair[1]
        low = row_ids(self.sub) % 2 == 0
        value = value + jnp.where(low, roll(value, -1, 0), roll(value, 1, 0))
        return pair_sum(value, 4) * 0.125


class Coarsest:
    def __init__(self, rows, cols):
        self.count, self.sub = rows // 2, cols * 2
        self.cells = range(self.count)
        self.scale = 0.25**3

    def pack(self, ref):
        low = lane_ids(self.sub) // 4 % 2 == 0
        parts = [ref[pl.ds(r * self.sub * 2, self.sub, stride=2), :] for r in range(2 * self.count)]
        return [jnp.where(low, parts[2 * g], parts[2 * g + 1]) for g in self.cells]

    def repeated(self, v, r):
        mine = lane_ids(self.sub) // 4 % 2 == r % 2
        return jnp.where(mine, v[r // 2], roll(v[r // 2], 4 if r % 2 == 0 else -4, 1))

    def lower_x(self, v, g):
        return jnp.where(lane_ids(self.sub) % 8 > 0, roll(v[g], 1, 1), roll(v[g - 1], -7, 1))

    def upper_x(self, v, g):
        after = v[(g + 1) % self.count]
        return jnp.where(lane_ids(self.sub) % 8 < 7, roll(v[g], -1, 1), roll(after, 7, 1))

    def faces(self, k):
        lane = lane_ids(self.sub)
        cx = [harmonic(self.lower_x(k, g), k[g], self.scale) for g in self.cells]
        out = []
        for g in self.cells:
            south = harmonic(roll(k[g], 1, 0), k[g], self.scale)
            under = jnp.where(lane < 8, 0.0, harmonic(roll(k[g], 8, 1), k[g], self.scale))
            over = jnp.where(lane >= 120, 0.0, roll(under, -8, 1))
            outer = 2.0 * k[g] * self.scale
            below, above = jnp.where(lane < 8, outer, under), jnp.where(lane >= 120, outer, over)
            east, north = self.upper_x(cx, g), roll(south, -1, 0)
            total = cx[g] + east + south + north + below + above
            weight = OMEGA / total
            out.append([weight * c for c in (cx[g], east, south, north, under, over)] + [weight])
        return out

    def solve(self, faces, rhs):
        start = [faces(g, 6) * rhs[g] for g in self.cells]

        def sweep(_, v):
            new = []
            for g in self.cells:
                side_x = faces(g, 0) * self.lower_x(v, g) + faces(g, 1) * self.upper_x(v, g)
                side_y = faces(g, 2) * roll(v[g], 1, 0) + faces(g, 3) * roll(v[g], -1, 0)
                side_z = faces(g, 4) * roll(v[g], 8, 1) + faces(g, 5) * roll(v[g], -8, 1)
                new.append(((1.0 - OMEGA) * v[g] + start[g] + side_z) + (side_x + side_y))
            return tuple(new)

        return lax.fori_loop(1, CSWEEPS, sweep, tuple(start))


class Exchange:
    def __init__(self, win, items, bufs, sems, base, ids):
        self.win, self.items, self.ids = win, items, ids
        self.ystage, self.yland, self.cstage, self.cland = bufs
        self.sems, self.base = sems, base
        self.layers = sum(h for _, h in items)

    def remote(self, src, dst, to):
        send, recv = self.sems
        copy = pltpu.make_async_remote_copy(
            src_ref=src, dst_ref=dst, send_sem=send.at[self.base], recv_sem=recv.at[self.base],
            device_id=to, device_id_type=MESH)
        self.base += 1
        copy.start()
        return copy

    def edge(self, h, side, i):
        ny, sub = self.win.ny, self.win.sub
        return (i, ny + i) if side == 0 else (ny - h + i, sub - h + i)

    def start(self):
        (me_r, me_c), near_r, near_c = self.ids
        nx, sub = self.win.nx, self.win.sub
        self.copies = []
        for side in (0, 1):
            n = 0
            for ref, h in self.items:
                for i in range(h):
                    mine, _ = self.edge(h, side, i)
                    self.ystage[side, n:n + nx, :] = ref[pl.ds(PAD * sub + mine, nx, stride=sub), :]
                    n += nx
            to = (me_r, near_c[side])
            self.copies.append(self.remote(self.ystage.at[side], self.yland.at[side], to))
        for ref, h in self.items:
            rows = h * sub
            for side, mine, theirs in ((0, PAD, PAD + nx), (1, PAD + nx - h, PAD - h)):
                self.copies.append(self.remote(
                    ref.at[pl.ds(mine * sub, rows), :], ref.at[pl.ds(theirs * sub, rows), :],
                    (near_r[side], me_c)))
        for xside in (0, 1):
            for side in (0, 1):
                n, slot = 0, 2 * xside + side
                for ref, h in self.items:
                    first = PAD if xside == 0 else PAD + nx - h
                    for i in range(h):
                        mine, _ = self.edge(h, side, i)
                        self.cstage[slot, n:n + h, :] = ref[pl.ds(first * sub + mine, h, stride=sub), :]
                        n += h
                to = (near_r[xside], near_c[side])
                self.copies.append(self.remote(self.cstage.at[slot], self.cland.at[slot], to))

    def finish(self):
        nx, sub = self.win.nx, self.win.sub
        for copy in self.copies:
            copy.wait()
        for side in (0, 1):
            n, m = 0, 0
            for ref, h in self.items:
                for i in range(h):
                    _, halo = self.edge(h, side, i)
                    ref[pl.ds(PAD * sub + halo, nx, stride=sub), :] = self.yland[side, n:n + nx, :]
                    n += nx
                    for xside, first in ((0, PAD + nx), (1, PAD - h)):
                        corner = self.cland[2 * xside + side, m:m + h, :]
                        ref[pl.ds(first * sub + halo, h, stride=sub), :] = corner
                    m += h


def stage_sizes(win, halos):
    layers = sum(halos)
    corner = sum(h * h for h in halos)
    corner = (corner + 7) // 8 * 8
    return [(2, layers * win.nx, 128)] * 2 + [(4, corner, 128)] * 2


def wrapped(value, size):
    return jnp.where(value >= size, value - size, value)


def others(sizes, ids, body):
    rows, cols = sizes
    me_r, me_c = ids[0]
    to_cols = [me_c] + [wrapped(me_c + cols - c, cols) for c in range(1, cols)]

    def row(r, carry):
        to_row = wrapped(me_r + rows - r, rows)
        for c in range(cols):
            body(r * cols + c, (to_row, to_cols[c]))
        return carry

    for c in range(1, cols):
        body(c, (me_r, to_cols[c]))
    lax.fori_loop(1, rows, row, 0, unroll=rows <= 8)


def gather(src, land, sems, sizes, ids):
    def one(slot, to):
        at = slot * 8 if isinstance(slot, int) else pl.multiple_of(slot * 8, 8)
        pltpu.make_async_remote_copy(
            src_ref=src, dst_ref=land.at[pl.ds(at, 8), :], send_sem=sems[0], recv_sem=sems[1],
            device_id=to, device_id_type=MESH).start()

    others(sizes, ids, one)


def gather_wait(land, tiles, sems, ids):
    (me_r, me_c), (left, _), _ = ids
    span = land.at[pl.ds(8, (tiles - 1) * 8), :]
    done = pltpu.make_async_remote_copy(
        src_ref=span, dst_ref=span, send_sem=sems[0], recv_sem=sems[1],
        device_id=(left, me_c), device_id_type=MESH)
    done.wait_send()
    done.wait_recv()


def cycle_kernel(sizes, wins, p_hbm, s_hbm, k_hbm, out, *scratch):
    rows, cols = sizes
    tiles = rows * cols
    fine, mid = wins
    scratch = list(scratch)

    def take(count):
        got, scratch[:count] = scratch[:count], []
        return got

    p_in, s_in, k_in, in_sems, out_sems = take(5)
    pw, pa, pb, sw, kw, vw = take(6)
    faces0 = take(5)
    b1, k1, va, vb, v1 = take(5)
    faces1 = take(5)
    k2, b2, b3, p2a, p2b = take(5)
    faces2 = take(5)
    faces3 = take(1)[0]
    tmp, tile_b, tile_k = take(3)
    send, recv, gsend, grecv = take(4)
    bufs = [take(4) for _ in range(6)]

    loads = []
    for i, (src, dst) in enumerate(((k_hbm, k_in), (p_hbm, p_in), (s_hbm, s_in))):
        loads.append(pltpu.make_async_copy(src, dst, in_sems.at[i]))
        loads[-1].start()

    me_r, me_c = lax.axis_index("row"), lax.axis_index("col")
    ids = ((me_r, me_c),
           (wrapped(me_r + rows - 1, rows), wrapped(me_r + 1, rows)),
           (wrapped(me_c + cols - 1, cols), wrapped(me_c + 1, cols)))

    barrier = pltpu.get_barrier_semaphore()
    others(sizes, ids, lambda _, to: pl.semaphore_signal(
        barrier, inc=1, device_id=to, device_id_type=MESH))

    nx, ny, sub = fine.nx, fine.ny, fine.sub

    def bring(pairs):
        def body(i, carry):
            for x in range(4):
                at = pl.ds(pl.multiple_of((4 * i + x + PAD) * sub, 8), ny)
                for src, dst in pairs:
                    dst[at, :] = src[4 * i + x]
            return carry

        lax.fori_loop(0, nx // 4, body, 0)

    base = 0

    def exchange(win, items, buf):
        nonlocal base
        made = Exchange(win, items, buf, (send, recv), base, ids)
        made.start()
        base = made.base
        return made

    loads[0].wait()
    bring([(k_in, kw)])
    loads[1].wait()
    loads[2].wait()
    bring([(p_in, pw), (s_in, sw)])
    pl.semaphore_wait(barrier, tiles - 1)
    halo_k = exchange(fine, [(kw, 3)], bufs[0])
    halo_p = exchange(fine, [(pw, 3), (sw, 2)], bufs[1])

    def halves(slot, value, n):
        at = slot * sub
        tmp[at:at + value.shape[0], :] = value
        return lambda: tmp[pl.ds(at, n, stride=2), :] + tmp[pl.ds(at + 1, n, stride=2), :]

    def to_mid(i, ref, sums):
        made = [halves(n, value, ny // 2) for n, value in enumerate(sums)]
        made = [value() * 0.125 for value in made]
        for n, value in enumerate(made):
            at = (i * len(sums) + n + PAD) * mid.sub
            ref[pl.ds(pl.multiple_of(at, 8), mid.ny), :] = value

    def k_mean(i, carry):
        to_mid(i, k1, [pair_sum(k_in[8 * i + 2 * n] + k_in[8 * i + 2 * n + 1], 1) for n in range(4)])
        return carry

    lax.fori_loop(0, nx // 8, k_mean, 0)

    def to_tile(values, tile):
        n = mid.ny // 2
        lane = lane_ids(n)
        made = [halves(x, pair_sum(values[2 * x] + values[2 * x + 1], 2), n) for x in range(mid.nx // 2)]
        made = [value() * 0.125 for value in made]
        for i in range(2):
            pack = made[i]
            for j in range(1, 4):
                pack = jnp.where(lane % 4 == j, made[2 * j + i], pack)
            tile[pl.ds(i, n, stride=2), :] = pack

    lo, hi, lo1, hi1 = PAD, PAD + nx, PAD, PAD + mid.nx
    to_tile([k1[mid.at(x), :] for x in range(lo1, hi1)], tile_k)
    k2[0:8, :] = tile_k[...]
    halo_k.finish()
    fine.faces(kw, *faces0, lo - 2, hi + 2, 6)
    halo_p.finish()
    halo_k1 = exchange(mid, [(k1, 3)], bufs[2])
    gather(tile_k, k2, (gsend.at[0], grecv.at[0]), sizes, ids)

    def put(win, ref):
        def store(x, value):
            ref[win.at(x), :] = value
        return store

    def put_both(x, value):
        pb[fine.at(x), :] = value

    fine.sweep(pw, sw, faces0, lo - 2, hi + 2, 9, put(fine, pa))
    fine.sweep(pa, sw, faces0, lo - 1, hi + 1, 9, put_both)

    def restrict0(i, carry):
        left = fine.residual([8 * i + PAD + n for n in range(8)], pb, sw, faces0)
        to_mid(i, b1, [pair_sum(left[2 * n] + left[2 * n + 1], 1) for n in range(4)])
        return carry

    lax.fori_loop(0, nx // 8, restrict0, 0)
    halo_b1 = exchange(mid, [(b1, 2)], bufs[3])

    def keep(win, src, dst):
        def body(i, carry):
            values = [src[win.at(4 * i + n + PAD), :] for n in range(4)]
            for n in range(4):
                dst[win.at(4 * i + n + PAD), :] = values[n]
            return carry

        lax.fori_loop(0, win.nx // 4, body, 0)

    keep(fine, pb, vw)
    halo_k1.finish()
    mid.faces(k1, *faces1, lo1 - 2, hi1 + 2, 10)
    coarse2, coarse3 = Packed(rows, cols), Coarsest(rows, cols)
    halo_b1.finish()

    def zero_sweep(xs):
        new = [faces1[4][mid.at(x), :] * b1[mid.at(x), :] for x in xs]
        for x, value in zip(xs, new):
            va[mid.at(x), :] = value

    mid.groups(lo1 - 2, hi1 + 2, 10, zero_sweep)
    mid.sweep(va, b1, faces1, lo1 - 1, hi1 + 1, 11, put(mid, vb))
    to_tile(mid.residual(list(range(lo1, hi1)), vb, b1, faces1), tile_b)
    b2[0:8, :] = tile_b[...]
    gather(tile_b, b2, (gsend.at[1], grecv.at[1]), sizes, ids)
    keep(mid, vb, v1)

    gather_wait(k2, tiles, (gsend.at[0], grecv.at[0]), ids)
    coarse2.faces(k2, *faces2)

    def k_coarsest(rs):
        new = [coarse2.block_mean(coarse2.landed(k2, r)) for r in rs]
        for r, value in zip(rs, new):
            b3[coarse2.at(r), :] = value

    coarse2.groups(k_coarsest)
    for g, group in enumerate(coarse3.faces(coarse3.pack(b3))):
        for side, value in enumerate(group):
            faces3[g, side] = value

    gather_wait(b2, tiles, (gsend.at[1], grecv.at[1]), ids)
    halo_v1 = exchange(mid, [(v1, 3)], bufs[4])
    halo_vw = exchange(fine, [(vw, 2)], bufs[5])
    coarse2.start(p2a, b2, faces2[4])
    coarse2.sweep(p2a, p2b, b2, faces2)

    def restrict2(rs):
        new = []
        for r, found in zip(rs, coarse2.beside(rs, p2b, *faces2[:3])):
            parts = zip(found, coarse2.load(faces2[3], r), coarse2.landed(b2, r))
            new.append(coarse2.block_mean([b - d * own + total for (own, total), d, b in parts]))
        for r, value in zip(rs, new):
            b3[coarse2.at(r), :] = value

    coarse2.groups(restrict2)
    e3 = coarse3.solve(lambda g, side: faces3[g, side], coarse3.pack(b3))
    for r in range(rows):
        value = coarse3.repeated(e3, r)
        for half in range(2):
            b3[pl.ds(r * coarse2.sub + half, coarse3.sub, stride=2), :] = value

    def correct2(rs):
        new = [[value + b3[coarse2.at(r), :] for value in coarse2.load(p2b, r)] for r in rs]
        for r, pair in zip(rs, new):
            coarse2.save(p2a, r, pair)

    coarse2.groups(correct2)
    coarse2.sweep(p2a, p2b, b2, faces2)
    coarse2.sweep(p2b, p2a, b2, faces2)

    halo_v1.finish()
    span = coarse2.sub
    lane = lane_ids(span)
    for dr, j in ((-1, 3), (0, 0), (0, 1), (0, 2), (0, 3), (1, 0)):
        for i, part in enumerate(coarse2.load(p2a, dr % rows)):
            part = pair_sum(pair_sum(jnp.where(lane % 4 == j, part, 0.0), 1), 2)
            turned = roll(part, 8 - span, 0)
            e = jnp.where(row_ids(8) < 6, part[0:8, :], turned[0:8, :])
            x = 2 * (8 * dr + 2 * j + i) + PAD
            for row in (x, x + 1):
                for half in range(2):
                    at = pl.ds(row * mid.sub + half, 8, stride=2)
                    va[at, :] = v1[at, :] + e
    mid.sweep(va, b1, faces1, lo1 - 2, hi1 + 2, 11, put(mid, vb))
    mid.sweep(vb, b1, faces1, lo1 - 1, hi1 + 1, 11, put(mid, va))

    halo_vw.finish()

    def correct0(g, carry):
        rs = [lo1 - 1 + 6 * g + n for n in range(6)]
        for n, r in enumerate(rs):
            e = va[mid.at(r), :]
            for half in range(2):
                tmp[pl.ds(n * sub + half, 8, stride=2), :] = e[0:8, :]
                tmp[pl.ds(n * sub + 16 + half, 2, stride=2), :] = e[8:10, :]
                tmp[pl.ds(n * sub + 20 + half, 2, stride=2), :] = e[14:16, :]
        new = []
        for n, r in enumerate(rs):
            e = tmp[n * sub:(n + 1) * sub, :]
            for x in (2 * r - PAD, 2 * r - PAD + 1):
                new.append((x, vw[fine.at(x), :] + e))
        for x, value in new:
            pa[fine.at(x), :] = value
        return carry

    lax.fori_loop(0, (mid.nx + 2) // 6, correct0, 0)
    fine.sweep(pa, sw, faces0, lo - 1, hi + 1, 9, put(fine, pb))

    def last(xs):
        rest = (1.0 - OMEGA) / OMEGA
        new = [rest * own + (sw[fine.at(x), :] + total) / faces0[3][fine.at(x), :]
               for x, (own, total) in zip(xs, fine.beside(xs, pb, *faces0[:3]))]
        for x, value in zip(xs, new):
            p_in[x - PAD] = value[0:ny, :]

    part = nx // 4
    writes = []
    for n in range(4):
        fine.groups(lo + n * part, lo + (n + 1) * part, part, last)
        span = pl.ds(n * part, part)
        writes.append(pltpu.make_async_copy(p_in.at[span], out.at[span], out_sems.at[n]))
        writes[-1].start()
    for write in writes:
        write.wait()


def on_device(sizes, pressure_in, source, permeability):
    rows, cols = sizes
    nx, ny, _ = pressure_in.shape
    fine, mid = Window(nx, ny, 1, 1.0), Window(nx // 2, ny // 2, 2, 0.25)

    def window(win):
        return pltpu.VMEM(((win.nx + 2 * PAD) * win.sub, 128), jnp.float32)

    packed = pltpu.VMEM((rows * cols * 8, 128), jnp.float32)
    halved = pltpu.VMEM((2, rows * cols * 4, 128), jnp.float32)
    scratch = [pltpu.VMEM(pressure_in.shape, jnp.float32)] * 3 + [pltpu.SemaphoreType.DMA((3,)), pltpu.SemaphoreType.DMA((4,))]
    scratch += [window(fine)] * 11 + [window(mid)] * 10 + [packed] * 3 + [halved] * 7
    scratch += [pltpu.VMEM((rows // 2, 7, cols * 2, 128), jnp.float32)]
    scratch += [pltpu.VMEM((8 * fine.sub, 128), jnp.float32)] + [pltpu.VMEM((8, 128), jnp.float32)] * 2
    scratch += [pltpu.SemaphoreType.DMA((64,))] * 2 + [pltpu.SemaphoreType.DMA((2,))] * 2
    for win, halos in ((fine, (3,)), (fine, (3, 2)), (mid, (3,)), (mid, (2,)), (mid, (3,)), (fine, (2,))):
        scratch += [pltpu.VMEM(size, jnp.float32) for size in stage_sizes(win, halos)]
    anywhere = pl.BlockSpec(memory_space=pl.ANY)
    scaled = pl.pallas_call(
        functools.partial(cycle_kernel, sizes, (fine, mid)),
        out_shape=jax.ShapeDtypeStruct(pressure_in.shape, jnp.float32),
        in_specs=[pl.BlockSpec(memory_space=pltpu.HBM)] * 3,
        out_specs=anywhere,
        scratch_shapes=scratch,
        compiler_params=pltpu.CompilerParams(
            collective_id=0, has_side_effects=True, vmem_limit_bytes=(24 if rows * cols <= 64 else 56) * 1024 * 1024),
    )(pressure_in, source, permeability)
    return OMEGA * scaled


def solution(mesh):
    sizes = (mesh.shape["row"], mesh.shape["col"])
    placed = (P("row", "col", None), P("row", "col", None), P("row", "col", None))
    return jax.shard_map(
        functools.partial(on_device, sizes), mesh=mesh, in_specs=placed,
        out_specs=P("row", "col", None), check_vma=False)
```

```python
import functools

import jax
import jax.numpy as jnp
from jax import lax
from jax.experimental import pallas as pl
from jax.experimental.pallas import tpu as pltpu
from jax.sharding import PartitionSpec as P

MESH = pl.DeviceIdType.MESH
OMEGA = 0.8
CSWEEPS = 16
PAD = 4


def lane_ids(rows):
    return lax.broadcasted_iota(jnp.int32, (rows, 128), 1)


def row_ids(rows):
    return lax.broadcasted_iota(jnp.int32, (rows, 128), 0)


def roll(value, shift, axis):
    return pltpu.roll(value, shift % value.shape[axis], axis)


def harmonic(left, right, scale):
    return (2.0 * scale) * left * right / (left + right)


def pair_sum(value, step):
    low = (lane_ids(value.shape[0]) // step) % 2 == 0
    return value + jnp.where(low, roll(value, -step, 1), roll(value, step, 1))


class Window:
    def __init__(self, nx, ny, step, scale):
        self.nx, self.ny, self.sub, self.step, self.scale = nx, ny, ny + 2 * PAD, step, scale

    def at(self, x):
        start = x * self.sub
        if not isinstance(x, int):
            start = pl.multiple_of(start, 8)
        return pl.ds(start, self.sub)

    def groups(self, lo, hi, most, body):
        count = -(-(hi - lo) // most)
        size = -(-(hi - lo) // count)

        def step(g, carry):
            start = jnp.minimum(lo + g * size, hi - size)
            body([start + i for i in range(size)])
            return carry

        lax.fori_loop(0, count, step, 0)

    def faces(self, perm, cx, cy, cz, diag, weight, lo, hi, most):
        lane = lane_ids(self.sub)

        def body(rows):
            ks = [perm[self.at(x), :] for x in [rows[0] - 1] + rows + [rows[-1] + 1]]
            west = [harmonic(k, other, self.scale) for k, other in zip(ks[:-1], ks[1:])]
            found = []
            for i, k in enumerate(ks[1:-1]):
                south = harmonic(roll(k, 1, 0), k, self.scale)
                under = harmonic(roll(k, self.step, 1), k, self.scale)
                under = jnp.where(lane < self.step, 0.0, under)
                outer = 2.0 * k * self.scale
                below = jnp.where(lane < self.step, outer, under)
                above = jnp.where(lane >= 128 - self.step, outer, roll(under, -self.step, 1))
                total = west[i] + west[i + 1] + south + roll(south, -1, 0) + below + above
                found.append((south, under, total, OMEGA / total))
            for x, lower, (south, under, total, inverse) in zip(rows, west, found):
                cx[self.at(x), :] = lower
                cy[self.at(x), :] = south
                cz[self.at(x), :] = under
                diag[self.at(x), :] = total
                weight[self.at(x), :] = inverse
            cx[self.at(rows[-1] + 1), :] = west[-1]

        self.groups(lo, hi, most, body)

    def beside(self, rows, v, cx, cy, cz):
        vs = [v[self.at(x), :] for x in [rows[0] - 1] + rows + [rows[-1] + 1]]
        west = [cx[self.at(x), :] for x in rows + [rows[-1] + 1]]
        out = []
        for i, x in enumerate(rows):
            own, south, under = vs[i + 1], cy[self.at(x), :], cz[self.at(x), :]
            total = west[i] * vs[i] + west[i + 1] * vs[i + 2]
            total = total + (south * roll(own, 1, 0) + roll(south * own, -1, 0))
            total = total + (under * roll(own, self.step, 1) + roll(under * own, -self.step, 1))
            out.append((own, total))
        return out

    def sweep(self, v, rhs, faces, lo, hi, most, store):
        cx, cy, cz, _, weight = faces

        def body(rows):
            new = [(1.0 - OMEGA) * own + weight[self.at(x), :] * (rhs[self.at(x), :] + total)
                   for x, (own, total) in zip(rows, self.beside(rows, v, cx, cy, cz))]
            for x, value in zip(rows, new):
                store(x, value)

        self.groups(lo, hi, most, body)

    def residual(self, rows, v, rhs, faces):
        cx, cy, cz, diag, _ = faces
        return [rhs[self.at(x), :] - diag[self.at(x), :] * own + total
                for x, (own, total) in zip(rows, self.beside(rows, v, cx, cy, cz))]


class Packed:
    def __init__(self, rows, cols):
        self.rows, self.cols, self.sub = rows, cols, cols * 4
        self.scale = 0.25**2

    def at(self, r):
        start = r * self.sub
        return pl.ds(start if isinstance(r, int) else pl.multiple_of(start, 8), self.sub)

    def landed(self, ref, r):
        start = pl.multiple_of(r * self.sub * 2, 8)
        return [ref[pl.ds(start + i, self.sub, stride=2), :] for i in range(2)]

    def load(self, ref, r):
        return [ref[i, self.at(r), :] for i in range(2)]

    def save(self, ref, r, pair):
        for i in range(2):
            ref[i, self.at(r), :] = pair[i]

    def west(self, before, here):
        j = lane_ids(self.sub) % 4
        return [jnp.where(j > 0, roll(here[1], 1, 1), roll(before[1], -3, 1)), here[0]]

    def east(self, here, after):
        j = lane_ids(self.sub) % 4
        return [here[1], jnp.where(j < 3, roll(here[0], -1, 1), roll(after[0], 3, 1))]

    def groups(self, body):
        size = 8 if self.rows % 8 == 0 else 1

        def step(g, carry):
            body([g * size + i for i in range(size)])
            return carry

        lax.fori_loop(0, self.rows // size, step, 0)

    def around(self, rows):
        return [lax.rem(rows[0] + self.rows - 1, self.rows)] + rows + [lax.rem(rows[-1] + 1, self.rows)]

    def faces(self, landed, cx, cy, cz, diag, weight):
        lane = lane_ids(self.sub)

        def first(rows):
            ks = [self.landed(landed, r) for r in self.around(rows)]
            new = [[harmonic(w, k, self.scale) for w, k in zip(self.west(before, here), here)]
                   for before, here in zip(ks, ks[1:-1])]
            for r, pair in zip(rows, new):
                self.save(cx, r, pair)

        self.groups(first)

        def second(rows):
            west = [self.load(cx, r) for r in self.around(rows)]
            found = []
            for n, r in enumerate(rows):
                east = self.east(west[n + 1], west[n + 2])
                both = []
                for i, k in enumerate(self.landed(landed, r)):
                    south = harmonic(roll(k, 1, 0), k, self.scale)
                    under = jnp.where(lane < 4, 0.0, harmonic(roll(k, 4, 1), k, self.scale))
                    outer = 2.0 * k * self.scale
                    below = jnp.where(lane < 4, outer, under)
                    above = jnp.where(lane >= 124, outer, roll(under, -4, 1))
                    total = west[n + 1][i] + east[i] + south + roll(south, -1, 0) + below + above
                    both.append((south, under, total, OMEGA / total))
                found.append(list(zip(*both)))
            for r, values in zip(rows, found):
                for ref, pair in zip((cy, cz, diag, weight), values):
                    self.save(ref, r, pair)

        self.groups(second)

    def beside(self, rows, v, cx, cy, cz):
        vs = [self.load(v, r) for r in self.around(rows)]
        west = [self.load(cx, r) for r in self.around(rows)]
        flow = [[c * value for c, value in zip(cs, both)] for cs, both in zip(west, vs)]
        out = []
        for n, r in enumerate(rows):
            lower, upper = self.west(vs[n], vs[n + 1]), self.east(flow[n + 1], flow[n + 2])
            souths, unders, pair = self.load(cy, r), self.load(cz, r), []
            for i in range(2):
                own, south, under = vs[n + 1][i], souths[i], unders[i]
                total = west[n + 1][i] * lower[i] + upper[i]
                total = total + (south * roll(own, 1, 0) + roll(south * own, -1, 0))
                total = total + (under * roll(own, 4, 1) + roll(under * own, -4, 1))
                pair.append((own, total))
            out.append(pair)
        return out

    def start(self, v, rhs, weight):
        def body(rows):
            new = [[w * b for w, b in zip(self.load(weight, r), self.landed(rhs, r))] for r in rows]
            for r, pair in zip(rows, new):
                self.save(v, r, pair)

        self.groups(body)

    def sweep(self, v, new, rhs, faces):
        cx, cy, cz, _, weight = faces

        def body(rows):
            values = []
            for r, found in zip(rows, self.beside(rows, v, cx, cy, cz)):
                parts = zip(found, self.load(weight, r), self.landed(rhs, r))
                values.append([(1.0 - OMEGA) * own + w * (b + total) for (own, total), w, b in parts])
            for r, pair in zip(rows, values):
                self.save(new, r, pair)

        self.groups(body)

    def block_mean(self, pair):
        value = pair[0] + pair[1]
        low = row_ids(self.sub) % 2 == 0
        value = value + jnp.where(low, roll(value, -1, 0), roll(value, 1, 0))
        return pair_sum(value, 4) * 0.125


class Coarsest:
    def __init__(self, rows, cols):
        self.count, self.sub = rows // 2, cols * 2
        self.cells = range(self.count)
        self.scale = 0.25**3

    def pack(self, ref):
        low = lane_ids(self.sub) // 4 % 2 == 0
        parts = [ref[pl.ds(r * self.sub * 2, self.sub, stride=2), :] for r in range(2 * self.count)]
        return [jnp.where(low, parts[2 * g], parts[2 * g + 1]) for g in self.cells]

    def repeated(self, v, r):
        mine = lane_ids(self.sub) // 4 % 2 == r % 2
        return jnp.where(mine, v[r // 2], roll(v[r // 2], 4 if r % 2 == 0 else -4, 1))

    def lower_x(self, v, g):
        return jnp.where(lane_ids(self.sub) % 8 > 0, roll(v[g], 1, 1), roll(v[g - 1], -7, 1))

    def upper_x(self, v, g):
        after = v[(g + 1) % self.count]
        return jnp.where(lane_ids(self.sub) % 8 < 7, roll(v[g], -1, 1), roll(after, 7, 1))

    def faces(self, k):
        lane = lane_ids(self.sub)
        cx = [harmonic(self.lower_x(k, g), k[g], self.scale) for g in self.cells]
        out = []
        for g in self.cells:
            south = harmonic(roll(k[g], 1, 0), k[g], self.scale)
            under = jnp.where(lane < 8, 0.0, harmonic(roll(k[g], 8, 1), k[g], self.scale))
            over = jnp.where(lane >= 120, 0.0, roll(under, -8, 1))
            outer = 2.0 * k[g] * self.scale
            below, above = jnp.where(lane < 8, outer, under), jnp.where(lane >= 120, outer, over)
            east, north = self.upper_x(cx, g), roll(south, -1, 0)
            total = cx[g] + east + south + north + below + above
            weight = OMEGA / total
            out.append([weight * c for c in (cx[g], east, south, north, under, over)] + [weight])
        return out

    def solve(self, faces, rhs):
        start = [faces(g, 6) * rhs[g] for g in self.cells]

        def sweep(_, v):
            new = []
            for g in self.cells:
                side_x = faces(g, 0) * self.lower_x(v, g) + faces(g, 1) * self.upper_x(v, g)
                side_y = faces(g, 2) * roll(v[g], 1, 0) + faces(g, 3) * roll(v[g], -1, 0)
                side_z = faces(g, 4) * roll(v[g], 8, 1) + faces(g, 5) * roll(v[g], -8, 1)
                new.append(((1.0 - OMEGA) * v[g] + start[g] + side_z) + (side_x + side_y))
            return tuple(new)

        return lax.fori_loop(1, CSWEEPS, sweep, tuple(start))


class Exchange:
    def __init__(self, win, items, bufs, sems, base, ids):
        self.win, self.items, self.ids = win, items, ids
        self.ystage, self.yland, self.cstage, self.cland = bufs
        self.sems, self.base = sems, base
        self.layers = sum(h for _, h in items)

    def remote(self, src, dst, to):
        send, recv = self.sems
        copy = pltpu.make_async_remote_copy(
            src_ref=src, dst_ref=dst, send_sem=send.at[self.base], recv_sem=recv.at[self.base],
            device_id=to, device_id_type=MESH)
        self.base += 1
        copy.start()
        return copy

    def edge(self, h, side, i):
        ny, sub = self.win.ny, self.win.sub
        return (i, ny + i) if side == 0 else (ny - h + i, sub - h + i)

    def start(self):
        (me_r, me_c), near_r, near_c = self.ids
        nx, sub = self.win.nx, self.win.sub
        self.copies = []
        for side in (0, 1):
            n = 0
            for ref, h in self.items:
                for i in range(h):
                    mine, _ = self.edge(h, side, i)
                    self.ystage[side, n:n + nx, :] = ref[pl.ds(PAD * sub + mine, nx, stride=sub), :]
                    n += nx
            to = (me_r, near_c[side])
            self.copies.append(self.remote(self.ystage.at[side], self.yland.at[side], to))
        for ref, h in self.items:
            rows = h * sub
            for side, mine, theirs in ((0, PAD, PAD + nx), (1, PAD + nx - h, PAD - h)):
                self.copies.append(self.remote(
                    ref.at[pl.ds(mine * sub, rows), :], ref.at[pl.ds(theirs * sub, rows), :],
                    (near_r[side], me_c)))
        for xside in (0, 1):
            for side in (0, 1):
                n, slot = 0, 2 * xside + side
                for ref, h in self.items:
                    first = PAD if xside == 0 else PAD + nx - h
                    for i in range(h):
                        mine, _ = self.edge(h, side, i)
                        self.cstage[slot, n:n + h, :] = ref[pl.ds(first * sub + mine, h, stride=sub), :]
                        n += h
                to = (near_r[xside], near_c[side])
                self.copies.append(self.remote(self.cstage.at[slot], self.cland.at[slot], to))

    def finish(self):
        nx, sub = self.win.nx, self.win.sub
        for copy in self.copies:
            copy.wait()
        for side in (0, 1):
            n, m = 0, 0
            for ref, h in self.items:
                for i in range(h):
                    _, halo = self.edge(h, side, i)
                    ref[pl.ds(PAD * sub + halo, nx, stride=sub), :] = self.yland[side, n:n + nx, :]
                    n += nx
                    for xside, first in ((0, PAD + nx), (1, PAD - h)):
                        corner = self.cland[2 * xside + side, m:m + h, :]
                        ref[pl.ds(first * sub + halo, h, stride=sub), :] = corner
                    m += h


def stage_sizes(win, halos):
    layers = sum(halos)
    corner = sum(h * h for h in halos)
    corner = (corner + 7) // 8 * 8
    return [(2, layers * win.nx, 128)] * 2 + [(4, corner, 128)] * 2


def wrapped(value, size):
    return jnp.where(value >= size, value - size, value)


def others(sizes, ids, body):
    rows, cols = sizes
    me_r, me_c = ids[0]
    to_cols = [me_c] + [wrapped(me_c + cols - c, cols) for c in range(1, cols)]

    def row(r, carry):
        to_row = wrapped(me_r + rows - r, rows)
        for c in range(cols):
            body(r * cols + c, (to_row, to_cols[c]))
        return carry

    for c in range(1, cols):
        body(c, (me_r, to_cols[c]))
    lax.fori_loop(1, rows, row, 0, unroll=rows <= 8)


def gather(src, land, sems, sizes, ids):
    def one(slot, to):
        at = slot * 8 if isinstance(slot, int) else pl.multiple_of(slot * 8, 8)
        pltpu.make_async_remote_copy(
            src_ref=src, dst_ref=land.at[pl.ds(at, 8), :], send_sem=sems[0], recv_sem=sems[1],
            device_id=to, device_id_type=MESH).start()

    others(sizes, ids, one)


def gather_wait(land, tiles, sems, ids):
    (me_r, me_c), (left, _), _ = ids
    span = land.at[pl.ds(8, (tiles - 1) * 8), :]
    done = pltpu.make_async_remote_copy(
        src_ref=span, dst_ref=span, send_sem=sems[0], recv_sem=sems[1],
        device_id=(left, me_c), device_id_type=MESH)
    done.wait_send()
    done.wait_recv()


def cycle_kernel(sizes, wins, p_hbm, s_hbm, k_hbm, out, *scratch):
    rows, cols = sizes
    tiles = rows * cols
    fine, mid = wins
    scratch = list(scratch)

    def take(count):
        got, scratch[:count] = scratch[:count], []
        return got

    p_in, s_in, k_in, in_sems, out_sems = take(5)
    pw, pa, pb, sw, kw, vw = take(6)
    faces0 = take(5)
    b1, k1, va, vb, v1 = take(5)
    faces1 = take(5)
    k2, b2, b3, p2a, p2b = take(5)
    faces2 = take(5)
    faces3 = take(1)[0]
    tmp, tile_b, tile_k = take(3)
    send, recv, gsend, grecv = take(4)
    bufs = [take(4) for _ in range(6)]

    loads = []
    for i, (src, dst) in enumerate(((k_hbm, k_in), (p_hbm, p_in), (s_hbm, s_in))):
        loads.append(pltpu.make_async_copy(src, dst, in_sems.at[i]))
        loads[-1].start()

    me_r, me_c = lax.axis_index("row"), lax.axis_index("col")
    ids = ((me_r, me_c),
           (wrapped(me_r + rows - 1, rows), wrapped(me_r + 1, rows)),
           (wrapped(me_c + cols - 1, cols), wrapped(me_c + 1, cols)))

    barrier = pltpu.get_barrier_semaphore()
    others(sizes, ids, lambda _, to: pl.semaphore_signal(
        barrier, inc=1, device_id=to, device_id_type=MESH))

    nx, ny, sub = fine.nx, fine.ny, fine.sub

    def bring(pairs):
        def body(i, carry):
            for x in range(4):
                at = pl.ds(pl.multiple_of((4 * i + x + PAD) * sub, 8), ny)
                for src, dst in pairs:
                    dst[at, :] = src[4 * i + x]
            return carry

        lax.fori_loop(0, nx // 4, body, 0)

    base = 0

    def exchange(win, items, buf):
        nonlocal base
        made = Exchange(win, items, buf, (send, recv), base, ids)
        made.start()
        base = made.base
        return made

    loads[0].wait()
    bring([(k_in, kw)])
    loads[1].wait()
    loads[2].wait()
    bring([(p_in, pw), (s_in, sw)])
    pl.semaphore_wait(barrier, tiles - 1)
    halo_k = exchange(fine, [(kw, 3)], bufs[0])
    halo_p = exchange(fine, [(pw, 3), (sw, 2)], bufs[1])

    def halves(slot, value, n):
        at = slot * sub
        tmp[at:at + value.shape[0], :] = value
        return lambda: tmp[pl.ds(at, n, stride=2), :] + tmp[pl.ds(at + 1, n, stride=2), :]

    def to_mid(i, ref, sums):
        made = [halves(n, value, ny // 2) for n, value in enumerate(sums)]
        made = [value() * 0.125 for value in made]
        for n, value in enumerate(made):
            at = (i * len(sums) + n + PAD) * mid.sub
            ref[pl.ds(pl.multiple_of(at, 8), mid.ny), :] = value

    def k_mean(i, carry):
        to_mid(i, k1, [pair_sum(k_in[8 * i + 2 * n] + k_in[8 * i + 2 * n + 1], 1) for n in range(4)])
        return carry

    lax.fori_loop(0, nx // 8, k_mean, 0)

    def to_tile(values, tile):
        n = mid.ny // 2
        lane = lane_ids(n)
        made = [halves(x, pair_sum(values[2 * x] + values[2 * x + 1], 2), n) for x in range(mid.nx // 2)]
        made = [value() * 0.125 for value in made]
        for i in range(2):
            pack = made[i]
            for j in range(1, 4):
                pack = jnp.where(lane % 4 == j, made[2 * j + i], pack)
            tile[pl.ds(i, n, stride=2), :] = pack

    lo, hi, lo1, hi1 = PAD, PAD + nx, PAD, PAD + mid.nx
    to_tile([k1[mid.at(x), :] for x in range(lo1, hi1)], tile_k)
    k2[0:8, :] = tile_k[...]
    halo_k.finish()
    fine.faces(kw, *faces0, lo - 2, hi + 2, 9)
    halo_p.finish()
    halo_k1 = exchange(mid, [(k1, 3)], bufs[2])
    gather(tile_k, k2, (gsend.at[0], grecv.at[0]), sizes, ids)

    def put(win, ref):
        def store(x, value):
            ref[win.at(x), :] = value
        return store

    def put_both(x, value):
        pb[fine.at(x), :] = value

    fine.sweep(pw, sw, faces0, lo - 2, hi + 2, 18, put(fine, pa))
    fine.sweep(pa, sw, faces0, lo - 1, hi + 1, 17, put_both)

    def restrict0(i, carry):
        left = fine.residual([16 * i + PAD + n for n in range(16)], pb, sw, faces0)
        to_mid(i, b1, [pair_sum(left[2 * n] + left[2 * n + 1], 1) for n in range(8)])
        return carry

    lax.fori_loop(0, nx // 16, restrict0, 0)
    halo_b1 = exchange(mid, [(b1, 2)], bufs[3])

    def keep(win, src, dst):
        def body(i, carry):
            values = [src[win.at(4 * i + n + PAD), :] for n in range(4)]
            for n in range(4):
                dst[win.at(4 * i + n + PAD), :] = values[n]
            return carry

        lax.fori_loop(0, win.nx // 4, body, 0)

    keep(fine, pb, vw)
    halo_k1.finish()
    mid.faces(k1, *faces1, lo1 - 2, hi1 + 2, 10)
    coarse2, coarse3 = Packed(rows, cols), Coarsest(rows, cols)
    halo_b1.finish()

    def zero_sweep(xs):
        new = [faces1[4][mid.at(x), :] * b1[mid.at(x), :] for x in xs]
        for x, value in zip(xs, new):
            va[mid.at(x), :] = value

    mid.groups(lo1 - 2, hi1 + 2, 10, zero_sweep)
    mid.sweep(va, b1, faces1, lo1 - 1, hi1 + 1, 11, put(mid, vb))
    to_tile(mid.residual(list(range(lo1, hi1)), vb, b1, faces1), tile_b)
    b2[0:8, :] = tile_b[...]
    gather(tile_b, b2, (gsend.at[1], grecv.at[1]), sizes, ids)
    keep(mid, vb, v1)

    gather_wait(k2, tiles, (gsend.at[0], grecv.at[0]), ids)
    coarse2.faces(k2, *faces2)

    def k_coarsest(rs):
        new = [coarse2.block_mean(coarse2.landed(k2, r)) for r in rs]
        for r, value in zip(rs, new):
            b3[coarse2.at(r), :] = value

    coarse2.groups(k_coarsest)
    for g, group in enumerate(coarse3.faces(coarse3.pack(b3))):
        for side, value in enumerate(group):
            faces3[g, side] = value

    gather_wait(b2, tiles, (gsend.at[1], grecv.at[1]), ids)
    halo_v1 = exchange(mid, [(v1, 3)], bufs[4])
    halo_vw = exchange(fine, [(vw, 2)], bufs[5])
    coarse2.start(p2a, b2, faces2[4])
    coarse2.sweep(p2a, p2b, b2, faces2)

    def restrict2(rs):
        new = []
        for r, found in zip(rs, coarse2.beside(rs, p2b, *faces2[:3])):
            parts = zip(found, coarse2.load(faces2[3], r), coarse2.landed(b2, r))
            new.append(coarse2.block_mean([b - d * own + total for (own, total), d, b in parts]))
        for r, value in zip(rs, new):
            b3[coarse2.at(r), :] = value

    coarse2.groups(restrict2)
    e3 = coarse3.solve(lambda g, side: faces3[g, side], coarse3.pack(b3))
    for r in range(rows):
        value = coarse3.repeated(e3, r)
        for half in range(2):
            b3[pl.ds(r * coarse2.sub + half, coarse3.sub, stride=2), :] = value

    def correct2(rs):
        new = [[value + b3[coarse2.at(r), :] for value in coarse2.load(p2b, r)] for r in rs]
        for r, pair in zip(rs, new):
            coarse2.save(p2a, r, pair)

    coarse2.groups(correct2)
    coarse2.sweep(p2a, p2b, b2, faces2)
    coarse2.sweep(p2b, p2a, b2, faces2)

    halo_v1.finish()
    span = coarse2.sub
    lane = lane_ids(span)
    for dr, j in ((-1, 3), (0, 0), (0, 1), (0, 2), (0, 3), (1, 0)):
        for i, part in enumerate(coarse2.load(p2a, dr % rows)):
            part = pair_sum(pair_sum(jnp.where(lane % 4 == j, part, 0.0), 1), 2)
            turned = roll(part, 8 - span, 0)
            e = jnp.where(row_ids(8) < 6, part[0:8, :], turned[0:8, :])
            x = 2 * (8 * dr + 2 * j + i) + PAD
            for row in (x, x + 1):
                for half in range(2):
                    at = pl.ds(row * mid.sub + half, 8, stride=2)
                    va[at, :] = v1[at, :] + e
    mid.sweep(va, b1, faces1, lo1 - 2, hi1 + 2, 11, put(mid, vb))
    mid.sweep(vb, b1, faces1, lo1 - 1, hi1 + 1, 11, put(mid, va))

    halo_vw.finish()

    def correct0(g, carry):
        rs = [lo1 - 1 + 6 * g + n for n in range(6)]
        for n, r in enumerate(rs):
            e = va[mid.at(r), :]
            for half in range(2):
                tmp[pl.ds(n * sub + half, 8, stride=2), :] = e[0:8, :]
                tmp[pl.ds(n * sub + 16 + half, 2, stride=2), :] = e[8:10, :]
                tmp[pl.ds(n * sub + 20 + half, 2, stride=2), :] = e[14:16, :]
        new = []
        for n, r in enumerate(rs):
            e = tmp[n * sub:(n + 1) * sub, :]
            for x in (2 * r - PAD, 2 * r - PAD + 1):
                new.append((x, vw[fine.at(x), :] + e))
        for x, value in new:
            pa[fine.at(x), :] = value
        return carry

    lax.fori_loop(0, (mid.nx + 2) // 6, correct0, 0)
    fine.sweep(pa, sw, faces0, lo - 1, hi + 1, 17, put(fine, pb))

    def last(xs):
        rest = (1.0 - OMEGA) / OMEGA
        new = [rest * own + (sw[fine.at(x), :] + total) / faces0[3][fine.at(x), :]
               for x, (own, total) in zip(xs, fine.beside(xs, pb, *faces0[:3]))]
        for x, value in zip(xs, new):
            p_in[x - PAD] = value[0:ny, :]

    part = nx // 2
    writes = []
    for n in range(2):
        fine.groups(lo + n * part, lo + (n + 1) * part, part, last)
        span = pl.ds(n * part, part)
        writes.append(pltpu.make_async_copy(p_in.at[span], out.at[span], out_sems.at[n]))
        writes[-1].start()
    for write in writes:
        write.wait()


def on_device(sizes, pressure_in, source, permeability):
    rows, cols = sizes
    nx, ny, _ = pressure_in.shape
    fine, mid = Window(nx, ny, 1, 1.0), Window(nx // 2, ny // 2, 2, 0.25)

    def window(win):
        return pltpu.VMEM(((win.nx + 2 * PAD) * win.sub, 128), jnp.float32)

    packed = pltpu.VMEM((rows * cols * 8, 128), jnp.float32)
    halved = pltpu.VMEM((2, rows * cols * 4, 128), jnp.float32)
    scratch = [pltpu.VMEM(pressure_in.shape, jnp.float32)] * 3 + [pltpu.SemaphoreType.DMA((3,)), pltpu.SemaphoreType.DMA((2,))]
    scratch += [window(fine)] * 11 + [window(mid)] * 10 + [packed] * 3 + [halved] * 7
    scratch += [pltpu.VMEM((rows // 2, 7, cols * 2, 128), jnp.float32)]
    scratch += [pltpu.VMEM((8 * fine.sub, 128), jnp.float32)] + [pltpu.VMEM((8, 128), jnp.float32)] * 2
    scratch += [pltpu.SemaphoreType.DMA((64,))] * 2 + [pltpu.SemaphoreType.DMA((2,))] * 2
    for win, halos in ((fine, (3,)), (fine, (3, 2)), (mid, (3,)), (mid, (2,)), (mid, (3,)), (fine, (2,))):
        scratch += [pltpu.VMEM(size, jnp.float32) for size in stage_sizes(win, halos)]
    anywhere = pl.BlockSpec(memory_space=pl.ANY)
    scaled = pl.pallas_call(
        functools.partial(cycle_kernel, sizes, (fine, mid)),
        out_shape=jax.ShapeDtypeStruct(pressure_in.shape, jnp.float32),
        in_specs=[pl.BlockSpec(memory_space=pltpu.HBM)] * 3,
        out_specs=anywhere,
        scratch_shapes=scratch,
        compiler_params=pltpu.CompilerParams(
            collective_id=0, has_side_effects=True, vmem_limit_bytes=56 * 1024 * 1024),
    )(pressure_in, source, permeability)
    return OMEGA * scaled


def solution(mesh):
    sizes = (mesh.shape["row"], mesh.shape["col"])
    placed = (P("row", "col", None), P("row", "col", None), P("row", "col", None))
    return jax.shard_map(
        functools.partial(on_device, sizes), mesh=mesh, in_specs=placed,
        out_specs=P("row", "col", None), check_vma=False)
```

```python
import functools

import jax
import jax.numpy as jnp
from jax import lax
from jax.experimental import pallas as pl
from jax.experimental.pallas import tpu as pltpu
from jax.sharding import PartitionSpec as P

MESH = pl.DeviceIdType.MESH
OMEGA = 0.8
CSWEEPS = 16
PAD = 4


def lane_ids(rows):
    return lax.broadcasted_iota(jnp.int32, (rows, 128), 1)


def row_ids(rows):
    return lax.broadcasted_iota(jnp.int32, (rows, 128), 0)


def roll(value, shift, axis):
    return pltpu.roll(value, shift % value.shape[axis], axis)


def harmonic(left, right, scale):
    return (2.0 * scale) * left * right / (left + right)


def pair_sum(value, step):
    low = (lane_ids(value.shape[0]) // step) % 2 == 0
    return value + jnp.where(low, roll(value, -step, 1), roll(value, step, 1))


class Window:
    def __init__(self, nx, ny, step, scale):
        self.nx, self.ny, self.sub, self.step, self.scale = nx, ny, ny + 2 * PAD, step, scale

    def at(self, x):
        start = x * self.sub
        if not isinstance(x, int):
            start = pl.multiple_of(start, 8)
        return pl.ds(start, self.sub)

    def groups(self, lo, hi, most, body):
        count = -(-(hi - lo) // most)
        size = -(-(hi - lo) // count)

        def step(g, carry):
            start = jnp.minimum(lo + g * size, hi - size)
            body([start + i for i in range(size)])
            return carry

        lax.fori_loop(0, count, step, 0)

    def faces(self, perm, cx, cy, cz, diag, weight, lo, hi, most):
        lane = lane_ids(self.sub)

        def body(rows):
            ks = [perm[self.at(x), :] for x in [rows[0] - 1] + rows + [rows[-1] + 1]]
            west = [harmonic(k, other, self.scale) for k, other in zip(ks[:-1], ks[1:])]
            found = []
            for i, k in enumerate(ks[1:-1]):
                south = harmonic(roll(k, 1, 0), k, self.scale)
                under = harmonic(roll(k, self.step, 1), k, self.scale)
                under = jnp.where(lane < self.step, 0.0, under)
                outer = 2.0 * k * self.scale
                below = jnp.where(lane < self.step, outer, under)
                above = jnp.where(lane >= 128 - self.step, outer, roll(under, -self.step, 1))
                total = west[i] + west[i + 1] + south + roll(south, -1, 0) + below + above
                found.append((south, under, total, OMEGA / total))
            for x, lower, (south, under, total, inverse) in zip(rows, west, found):
                cx[self.at(x), :] = lower
                cy[self.at(x), :] = south
                cz[self.at(x), :] = under
                diag[self.at(x), :] = total
                weight[self.at(x), :] = inverse
            cx[self.at(rows[-1] + 1), :] = west[-1]

        self.groups(lo, hi, most, body)

    def beside(self, rows, v, cx, cy, cz):
        vs = [v[self.at(x), :] for x in [rows[0] - 1] + rows + [rows[-1] + 1]]
        west = [cx[self.at(x), :] for x in rows + [rows[-1] + 1]]
        out = []
        for i, x in enumerate(rows):
            own, south, under = vs[i + 1], cy[self.at(x), :], cz[self.at(x), :]
            total = west[i] * vs[i] + west[i + 1] * vs[i + 2]
            total = total + (south * roll(own, 1, 0) + roll(south * own, -1, 0))
            total = total + (under * roll(own, self.step, 1) + roll(under * own, -self.step, 1))
            out.append((own, total))
        return out

    def sweep(self, v, rhs, faces, lo, hi, most, store):
        cx, cy, cz, _, weight = faces

        def body(rows):
            new = [(1.0 - OMEGA) * own + weight[self.at(x), :] * (rhs[self.at(x), :] + total)
                   for x, (own, total) in zip(rows, self.beside(rows, v, cx, cy, cz))]
            for x, value in zip(rows, new):
                store(x, value)

        self.groups(lo, hi, most, body)

    def residual(self, rows, v, rhs, faces):
        cx, cy, cz, diag, _ = faces
        return [rhs[self.at(x), :] - diag[self.at(x), :] * own + total
                for x, (own, total) in zip(rows, self.beside(rows, v, cx, cy, cz))]


class Packed:
    def __init__(self, rows, cols):
        self.rows, self.cols, self.sub = rows, cols, cols * 4
        self.scale = 0.25**2

    def at(self, r):
        start = r * self.sub
        return pl.ds(start if isinstance(r, int) else pl.multiple_of(start, 8), self.sub)

    def landed(self, ref, r):
        start = pl.multiple_of(r * self.sub * 2, 8)
        return [ref[pl.ds(start + i, self.sub, stride=2), :] for i in range(2)]

    def load(self, ref, r):
        return [ref[i, self.at(r), :] for i in range(2)]

    def save(self, ref, r, pair):
        for i in range(2):
            ref[i, self.at(r), :] = pair[i]

    def west(self, before, here):
        j = lane_ids(self.sub) % 4
        return [jnp.where(j > 0, roll(here[1], 1, 1), roll(before[1], -3, 1)), here[0]]

    def east(self, here, after):
        j = lane_ids(self.sub) % 4
        return [here[1], jnp.where(j < 3, roll(here[0], -1, 1), roll(after[0], 3, 1))]

    def groups(self, body):
        size = 8 if self.rows % 8 == 0 else 1

        def step(g, carry):
            body([g * size + i for i in range(size)])
            return carry

        lax.fori_loop(0, self.rows // size, step, 0)

    def around(self, rows):
        return [lax.rem(rows[0] + self.rows - 1, self.rows)] + rows + [lax.rem(rows[-1] + 1, self.rows)]

    def faces(self, landed, cx, cy, cz, diag, weight):
        lane = lane_ids(self.sub)

        def first(rows):
            ks = [self.landed(landed, r) for r in self.around(rows)]
            new = [[harmonic(w, k, self.scale) for w, k in zip(self.west(before, here), here)]
                   for before, here in zip(ks, ks[1:-1])]
            for r, pair in zip(rows, new):
                self.save(cx, r, pair)

        self.groups(first)

        def second(rows):
            west = [self.load(cx, r) for r in self.around(rows)]
            found = []
            for n, r in enumerate(rows):
                east = self.east(west[n + 1], west[n + 2])
                both = []
                for i, k in enumerate(self.landed(landed, r)):
                    south = harmonic(roll(k, 1, 0), k, self.scale)
                    under = jnp.where(lane < 4, 0.0, harmonic(roll(k, 4, 1), k, self.scale))
                    outer = 2.0 * k * self.scale
                    below = jnp.where(lane < 4, outer, under)
                    above = jnp.where(lane >= 124, outer, roll(under, -4, 1))
                    total = west[n + 1][i] + east[i] + south + roll(south, -1, 0) + below + above
                    both.append((south, under, total, OMEGA / total))
                found.append(list(zip(*both)))
            for r, values in zip(rows, found):
                for ref, pair in zip((cy, cz, diag, weight), values):
                    self.save(ref, r, pair)

        self.groups(second)

    def beside(self, rows, v, cx, cy, cz):
        vs = [self.load(v, r) for r in self.around(rows)]
        west = [self.load(cx, r) for r in self.around(rows)]
        flow = [[c * value for c, value in zip(cs, both)] for cs, both in zip(west, vs)]
        out = []
        for n, r in enumerate(rows):
            lower, upper = self.west(vs[n], vs[n + 1]), self.east(flow[n + 1], flow[n + 2])
            souths, unders, pair = self.load(cy, r), self.load(cz, r), []
            for i in range(2):
                own, south, under = vs[n + 1][i], souths[i], unders[i]
                total = west[n + 1][i] * lower[i] + upper[i]
                total = total + (south * roll(own, 1, 0) + roll(south * own, -1, 0))
                total = total + (under * roll(own, 4, 1) + roll(under * own, -4, 1))
                pair.append((own, total))
            out.append(pair)
        return out

    def start(self, v, rhs, weight):
        def body(rows):
            new = [[w * b for w, b in zip(self.load(weight, r), self.landed(rhs, r))] for r in rows]
            for r, pair in zip(rows, new):
                self.save(v, r, pair)

        self.groups(body)

    def sweep(self, v, new, rhs, faces):
        cx, cy, cz, _, weight = faces

        def body(rows):
            values = []
            for r, found in zip(rows, self.beside(rows, v, cx, cy, cz)):
                parts = zip(found, self.load(weight, r), self.landed(rhs, r))
                values.append([(1.0 - OMEGA) * own + w * (b + total) for (own, total), w, b in parts])
            for r, pair in zip(rows, values):
                self.save(new, r, pair)

        self.groups(body)

    def block_mean(self, pair):
        value = pair[0] + pair[1]
        low = row_ids(self.sub) % 2 == 0
        value = value + jnp.where(low, roll(value, -1, 0), roll(value, 1, 0))
        return pair_sum(value, 4) * 0.125


class Coarsest:
    def __init__(self, rows, cols):
        self.count, self.sub = rows // 2, cols * 2
        self.cells = range(self.count)
        self.scale = 0.25**3

    def pack(self, ref):
        low = lane_ids(self.sub) // 4 % 2 == 0
        parts = [ref[pl.ds(r * self.sub * 2, self.sub, stride=2), :] for r in range(2 * self.count)]
        return [jnp.where(low, parts[2 * g], parts[2 * g + 1]) for g in self.cells]

    def repeated(self, v, r):
        mine = lane_ids(self.sub) // 4 % 2 == r % 2
        return jnp.where(mine, v[r // 2], roll(v[r // 2], 4 if r % 2 == 0 else -4, 1))

    def lower_x(self, v, g):
        return jnp.where(lane_ids(self.sub) % 8 > 0, roll(v[g], 1, 1), roll(v[g - 1], -7, 1))

    def upper_x(self, v, g):
        after = v[(g + 1) % self.count]
        return jnp.where(lane_ids(self.sub) % 8 < 7, roll(v[g], -1, 1), roll(after, 7, 1))

    def faces(self, k):
        lane = lane_ids(self.sub)
        cx = [harmonic(self.lower_x(k, g), k[g], self.scale) for g in self.cells]
        out = []
        for g in self.cells:
            south = harmonic(roll(k[g], 1, 0), k[g], self.scale)
            under = jnp.where(lane < 8, 0.0, harmonic(roll(k[g], 8, 1), k[g], self.scale))
            over = jnp.where(lane >= 120, 0.0, roll(under, -8, 1))
            outer = 2.0 * k[g] * self.scale
            below, above = jnp.where(lane < 8, outer, under), jnp.where(lane >= 120, outer, over)
            east, north = self.upper_x(cx, g), roll(south, -1, 0)
            total = cx[g] + east + south + north + below + above
            weight = OMEGA / total
            out.append([weight * c for c in (cx[g], east, south, north, under, over)] + [weight])
        return out

    def solve(self, faces, rhs):
        start = [faces(g, 6) * rhs[g] for g in self.cells]

        def sweep(_, v):
            new = []
            for g in self.cells:
                side_x = faces(g, 0) * self.lower_x(v, g) + faces(g, 1) * self.upper_x(v, g)
                side_y = faces(g, 2) * roll(v[g], 1, 0) + faces(g, 3) * roll(v[g], -1, 0)
                side_z = faces(g, 4) * roll(v[g], 8, 1) + faces(g, 5) * roll(v[g], -8, 1)
                new.append(((1.0 - OMEGA) * v[g] + start[g] + side_z) + (side_x + side_y))
            return tuple(new)

        return lax.fori_loop(1, CSWEEPS, sweep, tuple(start))


class Exchange:
    def __init__(self, win, items, bufs, sems, base, ids):
        self.win, self.items, self.ids = win, items, ids
        self.ystage, self.yland, self.cstage, self.cland = bufs
        self.sems, self.base = sems, base
        self.layers = sum(h for _, h in items)

    def remote(self, src, dst, to):
        send, recv = self.sems
        copy = pltpu.make_async_remote_copy(
            src_ref=src, dst_ref=dst, send_sem=send.at[self.base], recv_sem=recv.at[self.base],
            device_id=to, device_id_type=MESH)
        self.base += 1
        copy.start()
        return copy

    def edge(self, h, side, i):
        ny, sub = self.win.ny, self.win.sub
        return (i, ny + i) if side == 0 else (ny - h + i, sub - h + i)

    def start(self):
        (me_r, me_c), near_r, near_c = self.ids
        nx, sub = self.win.nx, self.win.sub
        self.copies = []
        for side in (0, 1):
            n = 0
            for ref, h in self.items:
                for i in range(h):
                    mine, _ = self.edge(h, side, i)
                    self.ystage[side, n:n + nx, :] = ref[pl.ds(PAD * sub + mine, nx, stride=sub), :]
                    n += nx
            to = (me_r, near_c[side])
            self.copies.append(self.remote(self.ystage.at[side], self.yland.at[side], to))
        for ref, h in self.items:
            rows = h * sub
            for side, mine, theirs in ((0, PAD, PAD + nx), (1, PAD + nx - h, PAD - h)):
                self.copies.append(self.remote(
                    ref.at[pl.ds(mine * sub, rows), :], ref.at[pl.ds(theirs * sub, rows), :],
                    (near_r[side], me_c)))
        for xside in (0, 1):
            for side in (0, 1):
                n, slot = 0, 2 * xside + side
                for ref, h in self.items:
                    first = PAD if xside == 0 else PAD + nx - h
                    for i in range(h):
                        mine, _ = self.edge(h, side, i)
                        self.cstage[slot, n:n + h, :] = ref[pl.ds(first * sub + mine, h, stride=sub), :]
                        n += h
                to = (near_r[xside], near_c[side])
                self.copies.append(self.remote(self.cstage.at[slot], self.cland.at[slot], to))

    def finish(self):
        nx, sub = self.win.nx, self.win.sub
        for copy in self.copies:
            copy.wait()
        for side in (0, 1):
            n, m = 0, 0
            for ref, h in self.items:
                for i in range(h):
                    _, halo = self.edge(h, side, i)
                    ref[pl.ds(PAD * sub + halo, nx, stride=sub), :] = self.yland[side, n:n + nx, :]
                    n += nx
                    for xside, first in ((0, PAD + nx), (1, PAD - h)):
                        corner = self.cland[2 * xside + side, m:m + h, :]
                        ref[pl.ds(first * sub + halo, h, stride=sub), :] = corner
                    m += h


def stage_sizes(win, halos):
    layers = sum(halos)
    corner = sum(h * h for h in halos)
    corner = (corner + 7) // 8 * 8
    return [(2, layers * win.nx, 128)] * 2 + [(4, corner, 128)] * 2


def wrapped(value, size):
    return jnp.where(value >= size, value - size, value)


def along_cols(sizes, ids, body):
    (me_r, me_c), cols = ids[0], sizes[1]
    for c in range(1, cols):
        body(c, (me_r, wrapped(me_c + cols - c, cols)))


def along_rows(sizes, ids, body):
    (me_r, me_c), rows = ids[0], sizes[0]
    for r in range(1, rows):
        body(r, (wrapped(me_r + rows - r, rows), me_c))


def gather(src, land, sems, sizes, ids, stage):
    size = 8 if stage == 0 else 8 * sizes[1]

    def one(slot, to):
        pltpu.make_async_remote_copy(
            src_ref=src, dst_ref=land.at[pl.ds(slot * size, size), :], send_sem=sems[0].at[stage],
            recv_sem=sems[1].at[stage], device_id=to, device_id_type=MESH).start()

    (along_cols if stage == 0 else along_rows)(sizes, ids, one)


def gather_wait(land, sems, sizes, ids, stage):
    (me_r, me_c), (left, _), _ = ids
    rows, cols = sizes
    span = pl.ds(8, (cols - 1) * 8) if stage == 0 else pl.ds(cols * 8, (rows - 1) * cols * 8)
    done = pltpu.make_async_remote_copy(
        src_ref=land.at[span, :], dst_ref=land.at[span, :], send_sem=sems[0].at[stage],
        recv_sem=sems[1].at[stage], device_id=(left, me_c), device_id_type=MESH)
    done.wait_send()
    done.wait_recv()


def cycle_kernel(sizes, wins, p_hbm, s_hbm, k_hbm, out, *scratch):
    rows, cols = sizes
    fine, mid = wins
    scratch = list(scratch)

    def take(count):
        got, scratch[:count] = scratch[:count], []
        return got

    p_in, s_in, k_in, in_sems, out_sems = take(5)
    pw, pa, pb, sw, kw, vw = take(6)
    faces0 = take(5)
    b1, k1, va, vb, v1 = take(5)
    faces1 = take(5)
    k2, b2, b3, p2a, p2b = take(5)
    faces2 = take(5)
    faces3 = take(1)[0]
    tmp, tile_b, tile_k = take(3)
    send, recv, gsend, grecv = take(4)
    bufs = [take(4) for _ in range(6)]

    loads = []
    for i, (src, dst) in enumerate(((k_hbm, k_in), (p_hbm, p_in), (s_hbm, s_in))):
        loads.append(pltpu.make_async_copy(src, dst, in_sems.at[i]))
        loads[-1].start()

    me_r, me_c = lax.axis_index("row"), lax.axis_index("col")
    ids = ((me_r, me_c),
           (wrapped(me_r + rows - 1, rows), wrapped(me_r + 1, rows)),
           (wrapped(me_c + cols - 1, cols), wrapped(me_c + 1, cols)))

    barrier = pltpu.get_barrier_semaphore()
    def greet(_, to):
        pl.semaphore_signal(barrier, inc=1, device_id=to, device_id_type=MESH)

    for near_r in ids[1]:
        for near_c in ids[2]:
            greet(0, (near_r, near_c))
    along_cols(sizes, ids, greet)
    along_rows(sizes, ids, greet)

    nx, ny, sub = fine.nx, fine.ny, fine.sub

    def bring(pairs):
        def body(i, carry):
            for x in range(4):
                at = pl.ds(pl.multiple_of((4 * i + x + PAD) * sub, 8), ny)
                for src, dst in pairs:
                    dst[at, :] = src[4 * i + x]
            return carry

        lax.fori_loop(0, nx // 4, body, 0)

    base = 0

    def exchange(win, items, buf):
        nonlocal base
        made = Exchange(win, items, buf, (send, recv), base, ids)
        made.start()
        base = made.base
        return made

    loads[0].wait()
    bring([(k_in, kw)])
    loads[1].wait()
    loads[2].wait()
    bring([(p_in, pw), (s_in, sw)])
    pl.semaphore_wait(barrier, rows + cols + 2)
    halo_k = exchange(fine, [(kw, 3)], bufs[0])
    halo_p = exchange(fine, [(pw, 3), (sw, 2)], bufs[1])

    def halves(slot, value, n):
        at = slot * sub
        tmp[at:at + value.shape[0], :] = value
        return lambda: tmp[pl.ds(at, n, stride=2), :] + tmp[pl.ds(at + 1, n, stride=2), :]

    def to_mid(i, ref, sums):
        made = [halves(n, value, ny // 2) for n, value in enumerate(sums)]
        made = [value() * 0.125 for value in made]
        for n, value in enumerate(made):
            at = (i * len(sums) + n + PAD) * mid.sub
            ref[pl.ds(pl.multiple_of(at, 8), mid.ny), :] = value

    def k_mean(i, carry):
        to_mid(i, k1, [pair_sum(k_in[8 * i + 2 * n] + k_in[8 * i + 2 * n + 1], 1) for n in range(4)])
        return carry

    lax.fori_loop(0, nx // 8, k_mean, 0)

    def to_tile(values, tile):
        n = mid.ny // 2
        lane = lane_ids(n)
        made = [halves(x, pair_sum(values[2 * x] + values[2 * x + 1], 2), n) for x in range(mid.nx // 2)]
        made = [value() * 0.125 for value in made]
        for i in range(2):
            pack = made[i]
            for j in range(1, 4):
                pack = jnp.where(lane % 4 == j, made[2 * j + i], pack)
            tile[pl.ds(i, n, stride=2), :] = pack

    lo, hi, lo1, hi1 = PAD, PAD + nx, PAD, PAD + mid.nx
    to_tile([k1[mid.at(x), :] for x in range(lo1, hi1)], tile_k)
    k2[0:8, :] = tile_k[...]
    halo_k.finish()
    fine.faces(kw, *faces0, lo - 2, hi + 2, 9)
    halo_p.finish()
    halo_k1 = exchange(mid, [(k1, 3)], bufs[2])
    sems_k, sems_b = (gsend.at[0], grecv.at[0]), (gsend.at[1], grecv.at[1])
    gather(tile_k, k2, sems_k, sizes, ids, 0)

    def put(win, ref):
        def store(x, value):
            ref[win.at(x), :] = value
        return store

    def put_both(x, value):
        pb[fine.at(x), :] = value

    fine.sweep(pw, sw, faces0, lo - 2, hi + 2, 18, put(fine, pa))
    fine.sweep(pa, sw, faces0, lo - 1, hi + 1, 17, put_both)

    def restrict0(i, carry):
        left = fine.residual([16 * i + PAD + n for n in range(16)], pb, sw, faces0)
        to_mid(i, b1, [pair_sum(left[2 * n] + left[2 * n + 1], 1) for n in range(8)])
        return carry

    lax.fori_loop(0, nx // 16, restrict0, 0)
    halo_b1 = exchange(mid, [(b1, 2)], bufs[3])

    def keep(win, src, dst):
        def body(i, carry):
            values = [src[win.at(4 * i + n + PAD), :] for n in range(4)]
            for n in range(4):
                dst[win.at(4 * i + n + PAD), :] = values[n]
            return carry

        lax.fori_loop(0, win.nx // 4, body, 0)

    keep(fine, pb, vw)
    gather_wait(k2, sems_k, sizes, ids, 0)
    gather(k2.at[pl.ds(0, cols * 8), :], k2, sems_k, sizes, ids, 1)
    halo_k1.finish()
    mid.faces(k1, *faces1, lo1 - 2, hi1 + 2, 10)
    coarse2, coarse3 = Packed(rows, cols), Coarsest(rows, cols)
    halo_b1.finish()

    def zero_sweep(xs):
        new = [faces1[4][mid.at(x), :] * b1[mid.at(x), :] for x in xs]
        for x, value in zip(xs, new):
            va[mid.at(x), :] = value

    mid.groups(lo1 - 2, hi1 + 2, 10, zero_sweep)
    mid.sweep(va, b1, faces1, lo1 - 1, hi1 + 1, 11, put(mid, vb))
    to_tile(mid.residual(list(range(lo1, hi1)), vb, b1, faces1), tile_b)
    b2[0:8, :] = tile_b[...]
    gather(tile_b, b2, sems_b, sizes, ids, 0)
    keep(mid, vb, v1)

    gather_wait(b2, sems_b, sizes, ids, 0)
    gather(b2.at[pl.ds(0, cols * 8), :], b2, sems_b, sizes, ids, 1)
    gather_wait(k2, sems_k, sizes, ids, 1)
    coarse2.faces(k2, *faces2)

    def k_coarsest(rs):
        new = [coarse2.block_mean(coarse2.landed(k2, r)) for r in rs]
        for r, value in zip(rs, new):
            b3[coarse2.at(r), :] = value

    coarse2.groups(k_coarsest)
    for g, group in enumerate(coarse3.faces(coarse3.pack(b3))):
        for side, value in enumerate(group):
            faces3[g, side] = value

    gather_wait(b2, sems_b, sizes, ids, 1)
    halo_v1 = exchange(mid, [(v1, 3)], bufs[4])
    halo_vw = exchange(fine, [(vw, 2)], bufs[5])
    coarse2.start(p2a, b2, faces2[4])
    coarse2.sweep(p2a, p2b, b2, faces2)

    def restrict2(rs):
        new = []
        for r, found in zip(rs, coarse2.beside(rs, p2b, *faces2[:3])):
            parts = zip(found, coarse2.load(faces2[3], r), coarse2.landed(b2, r))
            new.append(coarse2.block_mean([b - d * own + total for (own, total), d, b in parts]))
        for r, value in zip(rs, new):
            b3[coarse2.at(r), :] = value

    coarse2.groups(restrict2)
    e3 = coarse3.solve(lambda g, side: faces3[g, side], coarse3.pack(b3))
    for r in range(rows):
        value = coarse3.repeated(e3, r)
        for half in range(2):
            b3[pl.ds(r * coarse2.sub + half, coarse3.sub, stride=2), :] = value

    def correct2(rs):
        new = [[value + b3[coarse2.at(r), :] for value in coarse2.load(p2b, r)] for r in rs]
        for r, pair in zip(rs, new):
            coarse2.save(p2a, r, pair)

    coarse2.groups(correct2)
    coarse2.sweep(p2a, p2b, b2, faces2)
    coarse2.sweep(p2b, p2a, b2, faces2)

    halo_v1.finish()
    span = coarse2.sub
    lane = lane_ids(span)
    for dr, j in ((-1, 3), (0, 0), (0, 1), (0, 2), (0, 3), (1, 0)):
        for i, part in enumerate(coarse2.load(p2a, dr % rows)):
            part = pair_sum(pair_sum(jnp.where(lane % 4 == j, part, 0.0), 1), 2)
            turned = roll(part, 8 - span, 0)
            e = jnp.where(row_ids(8) < 6, part[0:8, :], turned[0:8, :])
            x = 2 * (8 * dr + 2 * j + i) + PAD
            for row in (x, x + 1):
                for half in range(2):
                    at = pl.ds(row * mid.sub + half, 8, stride=2)
                    va[at, :] = v1[at, :] + e
    mid.sweep(va, b1, faces1, lo1 - 2, hi1 + 2, 11, put(mid, vb))
    mid.sweep(vb, b1, faces1, lo1 - 1, hi1 + 1, 11, put(mid, va))

    halo_vw.finish()

    def correct0(g, carry):
        rs = [lo1 - 1 + 6 * g + n for n in range(6)]
        for n, r in enumerate(rs):
            e = va[mid.at(r), :]
            for half in range(2):
                tmp[pl.ds(n * sub + half, 8, stride=2), :] = e[0:8, :]
                tmp[pl.ds(n * sub + 16 + half, 2, stride=2), :] = e[8:10, :]
                tmp[pl.ds(n * sub + 20 + half, 2, stride=2), :] = e[14:16, :]
        new = []
        for n, r in enumerate(rs):
            e = tmp[n * sub:(n + 1) * sub, :]
            for x in (2 * r - PAD, 2 * r - PAD + 1):
                new.append((x, vw[fine.at(x), :] + e))
        for x, value in new:
            pa[fine.at(x), :] = value
        return carry

    lax.fori_loop(0, (mid.nx + 2) // 6, correct0, 0)
    fine.sweep(pa, sw, faces0, lo - 1, hi + 1, 17, put(fine, pb))

    def last(xs):
        rest = (1.0 - OMEGA) / OMEGA
        new = [rest * own + (sw[fine.at(x), :] + total) / faces0[3][fine.at(x), :]
               for x, (own, total) in zip(xs, fine.beside(xs, pb, *faces0[:3]))]
        for x, value in zip(xs, new):
            p_in[x - PAD] = value[0:ny, :]

    part = nx // 2
    writes = []
    for n in range(2):
        fine.groups(lo + n * part, lo + (n + 1) * part, part, last)
        span = pl.ds(n * part, part)
        writes.append(pltpu.make_async_copy(p_in.at[span], out.at[span], out_sems.at[n]))
        writes[-1].start()
    for write in writes:
        write.wait()


def on_device(sizes, pressure_in, source, permeability):
    rows, cols = sizes
    nx, ny, _ = pressure_in.shape
    fine, mid = Window(nx, ny, 1, 1.0), Window(nx // 2, ny // 2, 2, 0.25)

    def window(win):
        return pltpu.VMEM(((win.nx + 2 * PAD) * win.sub, 128), jnp.float32)

    packed = pltpu.VMEM((rows * cols * 8, 128), jnp.float32)
    halved = pltpu.VMEM((2, rows * cols * 4, 128), jnp.float32)
    scratch = [pltpu.VMEM(pressure_in.shape, jnp.float32)] * 3 + [pltpu.SemaphoreType.DMA((3,)), pltpu.SemaphoreType.DMA((2,))]
    scratch += [window(fine)] * 11 + [window(mid)] * 10 + [packed] * 3 + [halved] * 7
    scratch += [pltpu.VMEM((rows // 2, 7, cols * 2, 128), jnp.float32)]
    scratch += [pltpu.VMEM((8 * fine.sub, 128), jnp.float32)] + [pltpu.VMEM((8, 128), jnp.float32)] * 2
    scratch += [pltpu.SemaphoreType.DMA((64,))] * 2 + [pltpu.SemaphoreType.DMA((2, 2))] * 2
    for win, halos in ((fine, (3,)), (fine, (3, 2)), (mid, (3,)), (mid, (2,)), (mid, (3,)), (fine, (2,))):
        scratch += [pltpu.VMEM(size, jnp.float32) for size in stage_sizes(win, halos)]
    anywhere = pl.BlockSpec(memory_space=pl.ANY)
    scaled = pl.pallas_call(
        functools.partial(cycle_kernel, sizes, (fine, mid)),
        out_shape=jax.ShapeDtypeStruct(pressure_in.shape, jnp.float32),
        in_specs=[pl.BlockSpec(memory_space=pltpu.HBM)] * 3,
        out_specs=anywhere,
        scratch_shapes=scratch,
        compiler_params=pltpu.CompilerParams(
            collective_id=0, has_side_effects=True, vmem_limit_bytes=56 * 1024 * 1024),
    )(pressure_in, source, permeability)
    return OMEGA * scaled


def solution(mesh):
    sizes = (mesh.shape["row"], mesh.shape["col"])
    placed = (P("row", "col", None), P("row", "col", None), P("row", "col", None))
    return jax.shard_map(
        functools.partial(on_device, sizes), mesh=mesh, in_specs=placed,
        out_specs=P("row", "col", None), check_vma=False)
```
